32 devices in a mesh: dp: 4 (over x, core), context: 8 (over z, y).
Axes of the slice: x: 2, y: 2, z: 4, core: 2. Of those that a mesh axis runs over, the one named last changes fastest.
Arguments:
- inputs: bfloat16 [4, 4096, 1024], P('dp', 'context'), may hold values from -6 to 6
- step_size: float32 [4, 4096], P('dp', 'context'), may hold values from 0.25 to 4099
- decay_rate: float32 [256], replicated, may hold values from 4.8828125e-05 to 0.125
- frequency: float32 [256], replicated, may hold values from -0.5 to 0.5
- input_proj: bfloat16 [1024, 512], replicated, may hold values from -0.1875 to 0.1875
- output_proj: bfloat16 [1024, 512], replicated, may hold values from -0.25 to 0.25
- skip_gain: float32 [1024], replicated, may hold values from 0.25 to 1.75
- cotangent: bfloat16 [4, 4096, 1024], P('dp', 'context'), may hold values from -6 to 6
Outputs:
- outputs: bfloat16 [4, 4096, 1024], P('dp', 'context')
- input_grad: bfloat16 [4, 4096, 1024], P('dp', 'context')
- input_proj_grad: float32 [1024, 512], P('context')
- output_proj_grad: float32 [1024, 512], P('context')
The draws below stay inside these ranges and needn't reach their ends.
All inputs are finite; a program needn't handle non-finite values.
Results may differ from the reference program's by a relative error of at most 0.0036.
Values sent between devices are 32-bit elements; how exact they have to be, the bound alone decides.
No kernel may reach another device: no remote copies, remote signals or barrier semaphores. Data moves between devices by JAX's collectives and lax.ppermute only.
A program may use at most 64 MiB of HBM per device.

```python
import math
import jax
import jax.numpy as jnp
from jax import lax

H = 1024
P_SIZE = 256
L_DEV = 512
SEQS = 4
SEQUENCE_LENGTH = 4096


def draw_step_size(key, part):
    key_base, key_scale, key_first, key_offset = jax.random.split(key, 4)
    block_count = SEQUENCE_LENGTH // L_DEV
    base_steps = jax.random.uniform(key_base, (SEQS, SEQUENCE_LENGTH), jnp.float32, 0.5, 1.5)
    block_scale = jax.random.uniform(key_scale, (SEQS, block_count), jnp.float32, 0.6, 1.4)
    rescaled_values = base_steps * jnp.repeat(block_scale, L_DEV, axis=1)
    leading_position = jax.random.randint(key_first, (SEQS, 1), 0, SEQUENCE_LENGTH)
    offset_spot = jax.random.randint(key_offset, (SEQS, 1), 1, SEQUENCE_LENGTH)
    trailing_position = (leading_position + offset_spot) % SEQUENCE_LENGTH
    token_places = jnp.arange(SEQUENCE_LENGTH, dtype=jnp.int32)[None, :]
    event_marks = (token_places == leading_position).astype(jnp.float32) + (token_places == trailing_position).astype(jnp.float32)
    return rescaled_values + float(SEQUENCE_LENGTH) * event_marks


def draw_decay_rate(key, part):
    key_pick, key_slow, key_fast = jax.random.split(key, 3)
    slow_share = 0.5
    slow_pick = jax.random.uniform(key_pick, (P_SIZE,), jnp.float32) < slow_share
    slow_rates = jnp.exp(jax.random.uniform(key_slow, (P_SIZE,), jnp.float32, math.log(0.2), math.log(0.6))) / float(SEQUENCE_LENGTH)
    fast_rates = jnp.exp(jax.random.uniform(key_fast, (P_SIZE,), jnp.float32, math.log(1.0 / 40.0), math.log(1.0 / 8.0)))
    return jnp.where(slow_pick, slow_rates, fast_rates)


def spiked(drawn, own_key, source, target, parts, factor):
    def block_of(axis_at):
        return (jnp.arange(drawn.shape[axis_at]) // (drawn.shape[axis_at] // parts)).reshape((-1,) + (1,) * (drawn.ndim - 1 - axis_at))

    first = jax.random.permutation(own_key, parts)[block_of(target)]
    other_side = (block_of(target) + parts // 2) % parts
    return jnp.where((block_of(source) == first) | (block_of(source) == other_side), factor * drawn, drawn)


def shard_levels(own_key, dims, cuts, smallest, largest):
    factor_of, own = 1.0, jax.random.fold_in(own_key, 6)
    for axis_at, parts in cuts:
        draws = jnp.exp(jax.random.uniform(jax.random.fold_in(own, axis_at), (parts,), jnp.float32, smallest / len(cuts), largest / len(cuts)))
        factor_of = factor_of * jnp.repeat(draws, dims[axis_at] // parts).reshape([-1 if axis == axis_at else 1 for axis in range(len(dims))])
    return factor_of


def centred(stream_key, extent, deviation, limit, cuts=(), kind=jnp.bfloat16):
    array = jax.random.normal(stream_key, extent, jnp.float32) * deviation
    if len(cuts) > 0:
        array = shard_levels(stream_key, extent, cuts, -0.22, 0.18) * array
    return jnp.clip(array, min=-limit, max=limit).astype(kind)


def heavy_noise(rng, extent, spread, most, shards, heavy, kind=jnp.bfloat16):
    drawn = spread * jax.random.normal(rng, extent, jnp.float32)
    if shards:
        drawn = drawn * shard_levels(rng, extent, shards, -0.22, 0.18)
    return jnp.clip(spiked(drawn, jax.random.fold_in(rng, 3), *heavy), -most, most).astype(kind)


def setup_inputs(seed: int = 0) -> dict:
    key_of = jax.random.split(jax.random.key(seed), 9)
    return {
        "inputs": heavy_noise(key_of[0], (SEQS, SEQUENCE_LENGTH, H), 1.0, 6.0, ((0, 4), (1, 8)), (1, 2, 8, 2.0)),
        "step_size": draw_step_size(jax.random.fold_in(key_of[8], 71), 0),
        "decay_rate": draw_decay_rate(jax.random.fold_in(key_of[8], 71), 0),
        "frequency": jnp.clip(jax.random.uniform(key_of[3], (P_SIZE,), jnp.float32, -0.5, 0.5), -0.5, 0.5),
        "input_proj": centred(key_of[4], (H, 2 * P_SIZE), H ** -0.5, 0.1875),
        "output_proj": centred(key_of[5], (H, 2 * P_SIZE), (2 * P_SIZE) ** -0.5, 0.25),
        "skip_gain": jnp.clip(1.0 + 0.15 * jax.random.normal(key_of[6], (H,), jnp.float32), 0.25, 1.75),
        "cotangent": heavy_noise(key_of[7], (SEQS, SEQUENCE_LENGTH, H), 1.0, 6.0, ((0, 4), (1, 8)), (1, 2, 8, 2.0)),
    }


def sequence_pass(inputs_row, step_row, cotangent_row, decay_rate, frequency, input_proj, output_proj, skip_gain):
    damping = jnp.exp(-step_row[:, None] * decay_rate)
    phase_turn = step_row[:, None] * frequency
    lam_re = damping * jnp.cos(phase_turn)
    lam_im = damping * jnp.sin(phase_turn)
    norm_gain = jnp.sqrt(-jnp.expm1(-2.0 * decay_rate))
    pair_gain = jnp.concatenate([norm_gain, norm_gain])
    state_count = decay_rate.shape[0]
    drive_term = jnp.dot(inputs_row, input_proj, preferred_element_type=jnp.float32) * pair_gain

    def forward_step(carry_pair, slice_pack):
        carry_re, carry_im = carry_pair
        step_re, step_im, push_re, push_im = slice_pack
        new_re = step_re * carry_re - step_im * carry_im + push_re
        new_im = step_re * carry_im + step_im * carry_re + push_im
        return ((new_re, new_im), (new_re, new_im))
    start_pair = (jnp.zeros((state_count,), jnp.float32), jnp.zeros((state_count,), jnp.float32))
    _, (state_re, state_im) = lax.scan(forward_step, start_pair, (lam_re, lam_im, drive_term[:, :state_count], drive_term[:, state_count:]))
    state_pairs = jnp.concatenate([state_re, state_im], axis=1).astype(jnp.bfloat16)
    mixed = jnp.dot(state_pairs, output_proj.T, preferred_element_type=jnp.float32)
    outputs = (mixed + skip_gain * inputs_row.astype(jnp.float32)).astype(jnp.bfloat16)
    adjoint_drive = jnp.dot(cotangent_row, output_proj, preferred_element_type=jnp.float32)
    next_re = jnp.concatenate([lam_re[1:], jnp.zeros_like(lam_re[:1])], axis=0)
    next_im = jnp.concatenate([lam_im[1:], jnp.zeros_like(lam_im[:1])], axis=0)

    def backward_update(carry_pair, slice_pack):
        carry_re, carry_im = carry_pair
        step_re, step_im, push_re, push_im = slice_pack
        new_re = push_re + step_re * carry_re + step_im * carry_im
        new_im = push_im + step_re * carry_im - step_im * carry_re
        return ((new_re, new_im), (new_re, new_im))
    _, (back_re, back_im) = lax.scan(backward_update, start_pair, (next_re, next_im, adjoint_drive[:, :state_count], adjoint_drive[:, state_count:]), reverse=True)
    adjoint_pairs = (jnp.concatenate([back_re, back_im], axis=1) * pair_gain).astype(jnp.bfloat16)
    back_in = jnp.dot(adjoint_pairs, input_proj.T, preferred_element_type=jnp.float32)
    input_grad = (back_in + skip_gain * cotangent_row.astype(jnp.float32)).astype(jnp.bfloat16)
    grad_in_term = jnp.dot(inputs_row.T, adjoint_pairs, preferred_element_type=jnp.float32)
    grad_out_term = jnp.dot(cotangent_row.T, state_pairs, preferred_element_type=jnp.float32)
    return (outputs, input_grad, grad_in_term, grad_out_term)

def reference(inputs, step_size, decay_rate, frequency, input_proj, output_proj, skip_gain, cotangent):

    def one_sequence(seq_pack):
        return sequence_pass(seq_pack[0], seq_pack[1], seq_pack[2], decay_rate, frequency, input_proj, output_proj, skip_gain)
    outputs, input_grad, grad_in_terms, grad_out_terms = lax.map(one_sequence, (inputs, step_size, cotangent))
    grad_scale = float(SEQS * SEQUENCE_LENGTH) ** (-0.5)
    input_proj_grad = lax.optimization_barrier(jnp.sum(grad_in_terms, axis=0)) * grad_scale
    output_proj_grad = lax.optimization_barrier(jnp.sum(grad_out_terms, axis=0)) * grad_scale
    return (outputs, input_grad, input_proj_grad, output_proj_grad)
```

```python
import functools

import jax
import jax.numpy as jnp
from jax import lax
from jax.experimental import pallas as pl
from jax.experimental.pallas import tpu as pltpu
from jax.sharding import PartitionSpec as P

CHUNKS = 8
LANES = 128
VMEM_LIMIT = 24 * 1024 * 1024

TWO_OVER_PI = 0.6366197723675814
PIO2_HIGH = 1.5703125
PIO2_MID = 0.0004837512969970703
PIO2_LOW = 7.549789948768648e-08


def sin_cos(angle):
    quadrant_real = jnp.floor(angle * TWO_OVER_PI + 0.5)
    rest = angle - quadrant_real * PIO2_HIGH
    rest = rest - quadrant_real * PIO2_MID
    rest = rest - quadrant_real * PIO2_LOW
    square = rest * rest
    sine = rest + rest * square * (
        -1.6666654611e-1 + square * (8.3321608736e-3 + square * -1.9515295891e-4)
    )
    cosine = (
        1.0
        - 0.5 * square
        + square
        * square
        * (4.166664568298827e-2 + square * (-1.388731625493765e-3 + square * 2.443315711809948e-5))
    )
    quadrant = quadrant_real.astype(jnp.int32)
    swapped = (quadrant & 1) == 1
    sin_base = jnp.where(swapped, cosine, sine)
    cos_base = jnp.where(swapped, sine, cosine)
    sin_value = jnp.where((quadrant & 2) == 2, -sin_base, sin_base)
    cos_value = jnp.where(((quadrant + 1) & 2) == 2, -cos_base, cos_base)
    return sin_value, cos_value


def gain_of(decay):
    twice = 2.0 * decay
    series = 1.0 / 3628800.0
    for factorial in (362880.0, 40320.0, 5040.0, 720.0, 120.0, 24.0, 6.0, 2.0, 1.0):
        series = 1.0 / factorial - twice * series
    return jnp.sqrt(jnp.where(twice < 0.5, twice * series, 1.0 - jnp.exp(-twice)))


def local_scan_kernel(
    step_ref,
    decay_ref,
    frequency_ref,
    in_hbm,
    cot_hbm,
    in_proj_hbm,
    out_proj_hbm,
    fwd_re,
    fwd_im,
    fwd_are,
    fwd_aim,
    back_re,
    back_im,
    back_are,
    back_aim,
    chunk_ref,
    summary_ref,
    in_vmem,
    cot_vmem,
    in_proj_vmem,
    out_proj_vmem,
    lam_re,
    lam_im,
    drive,
    adjoint,
    sems,
):
    rows = in_vmem.shape[0]
    length = rows // CHUNKS
    states = decay_ref.shape[1]
    lanes = states // LANES
    loads = [
        pltpu.make_async_copy(source, target, sems.at[slot])
        for slot, (source, target) in enumerate(
            (
                (in_hbm, in_vmem),
                (in_proj_hbm, in_proj_vmem),
                (cot_hbm, cot_vmem),
                (out_proj_hbm, out_proj_vmem),
            )
        )
    ]
    for load in loads:
        load.start()
    decay = decay_ref[...]
    frequency = frequency_ref[...]
    gain = gain_of(decay)
    steps = step_ref[...]
    for place in range(length):
        here = jnp.broadcast_to(steps[:, place : place + 1], (CHUNKS, states))
        damping = jnp.exp(-here * decay)
        sine, cosine = sin_cos(here * frequency)
        lam_re[pl.ds(place * CHUNKS, CHUNKS), :] = damping * cosine
        lam_im[pl.ds(place * CHUNKS, CHUNKS), :] = damping * sine
    loads[0].wait()
    loads[1].wait()
    pair_gain = jnp.concatenate([gain, gain], axis=1)
    driven = (
        jnp.dot(in_vmem[...], in_proj_vmem[...], preferred_element_type=jnp.float32) * pair_gain
    )
    for lane in range(2 * lanes):
        drive[lane] = driven[:, lane * LANES : (lane + 1) * LANES]
    loads[2].wait()
    loads[3].wait()
    driven = jnp.dot(cot_vmem[...], out_proj_vmem[...], preferred_element_type=jnp.float32)
    for lane in range(2 * lanes):
        adjoint[lane] = driven[:, lane * LANES : (lane + 1) * LANES]

    def gather(ref, first, spread):
        return jnp.concatenate([ref[first + lane, spread, :] for lane in range(lanes)], axis=1)

    def scatter(ref, spread, value):
        for lane in range(lanes):
            ref[lane, spread, :] = value[:, lane * LANES : (lane + 1) * LANES]

    def body(place, carry):
        f_are, f_aim, f_re, f_im, b_are, b_aim, b_re, b_im = carry
        tile = pl.ds(pl.multiple_of(place * CHUNKS, CHUNKS), CHUNKS)
        spread = pl.ds(place, CHUNKS, stride=length)
        l_re, l_im = lam_re[tile, :], lam_im[tile, :]
        new_are = l_re * f_are - l_im * f_aim
        new_aim = l_re * f_aim + l_im * f_are
        new_re = l_re * f_re - l_im * f_im + gather(drive, 0, spread)
        new_im = l_re * f_im + l_im * f_re + gather(drive, lanes, spread)
        scatter(fwd_are, spread, new_are)
        scatter(fwd_aim, spread, new_aim)
        scatter(fwd_re, spread, new_re)
        scatter(fwd_im, spread, new_im)
        mirror = length - 1 - place
        tile = pl.ds(pl.multiple_of(mirror * CHUNKS, CHUNKS), CHUNKS)
        spread = pl.ds(mirror, CHUNKS, stride=length)
        l_re, l_im = lam_re[tile, :], lam_im[tile, :]
        a_re = b_re + gather(adjoint, 0, spread)
        a_im = b_im + gather(adjoint, lanes, spread)
        scatter(back_are, spread, b_are)
        scatter(back_aim, spread, b_aim)
        scatter(back_re, spread, a_re)
        scatter(back_im, spread, a_im)
        next_are = l_re * b_are + l_im * b_aim
        next_aim = l_re * b_aim - l_im * b_are
        next_re = l_re * a_re + l_im * a_im
        next_im = l_re * a_im - l_im * a_re
        return (new_are, new_aim, new_re, new_im, next_are, next_aim, next_re, next_im)

    zero = jnp.zeros((CHUNKS, states), jnp.float32)
    one = jnp.ones((CHUNKS, states), jnp.float32)
    totals = lax.fori_loop(
        0, length, body, (one, zero, zero, zero, one, zero, zero, zero), unroll=4
    )
    a_re, a_im, f_re, f_im, _, _, b_re, b_im = totals
    for slot, part in enumerate((a_re, a_im, f_re, f_im, b_re, b_im)):
        chunk_ref[slot] = part
    row = lambda part, chunk: part[chunk : chunk + 1, :]
    t_are, t_aim = row(a_re, 0), row(a_im, 0)
    t_re, t_im = row(f_re, 0), row(f_im, 0)
    for chunk in range(1, CHUNKS):
        l_re, l_im = row(a_re, chunk), row(a_im, chunk)
        t_are, t_aim = l_re * t_are - l_im * t_aim, l_re * t_aim + l_im * t_are
        t_re, t_im = (
            l_re * t_re - l_im * t_im + row(f_re, chunk),
            l_re * t_im + l_im * t_re + row(f_im, chunk),
        )
    u_re, u_im = row(b_re, CHUNKS - 1), row(b_im, CHUNKS - 1)
    for chunk in range(CHUNKS - 2, -1, -1):
        l_re, l_im = row(a_re, chunk), row(a_im, chunk)
        u_re, u_im = (
            l_re * u_re + l_im * u_im + row(b_re, chunk),
            l_re * u_im - l_im * u_re + row(b_im, chunk),
        )
    summary_ref[...] = jnp.concatenate(
        [t_are, t_aim, t_re, t_im, u_re, u_im, t_re, t_re], axis=0
    )


def local_scan(step_rows, decay, frequency, flat_in, flat_cot, input_proj, output_proj):
    rows = flat_in.shape[0]
    states = decay.shape[1]
    lanes = states // LANES
    plane = jax.ShapeDtypeStruct((lanes, rows, LANES), jnp.float32)
    vmem = pl.BlockSpec(memory_space=pltpu.VMEM)
    anywhere = pl.BlockSpec(memory_space=pl.ANY)
    return pl.pallas_call(
        local_scan_kernel,
        out_shape=[plane] * 8
        + [
            jax.ShapeDtypeStruct((6, CHUNKS, states), jnp.float32),
            jax.ShapeDtypeStruct((8, states), jnp.float32),
        ],
        in_specs=[vmem] * 3 + [anywhere] * 4,
        out_specs=[vmem] * 10,
        scratch_shapes=[
            pltpu.VMEM(flat_in.shape, flat_in.dtype),
            pltpu.VMEM(flat_cot.shape, flat_cot.dtype),
            pltpu.VMEM(input_proj.shape, input_proj.dtype),
            pltpu.VMEM(output_proj.shape, output_proj.dtype),
            pltpu.VMEM((rows, states), jnp.float32),
            pltpu.VMEM((rows, states), jnp.float32),
            pltpu.VMEM((2 * lanes, rows, LANES), jnp.float32),
            pltpu.VMEM((2 * lanes, rows, LANES), jnp.float32),
            pltpu.SemaphoreType.DMA((4,)),
        ],
        compiler_params=pltpu.CompilerParams(vmem_limit_bytes=VMEM_LIMIT),
        cost_estimate=pl.CostEstimate(
            flops=4 * rows * flat_in.shape[1] * 2 * states,
            bytes_accessed=4 * 2**20,
            transcendentals=rows * states,
        ),
        name="local_scan",
    )(step_rows, decay, frequency, flat_in, flat_cot, input_proj, output_proj)


def states_kernel(
    device_count,
    where_ref,
    decay_ref,
    chunk_ref,
    fwd_re,
    fwd_im,
    fwd_are,
    fwd_aim,
    back_re,
    back_im,
    back_are,
    back_aim,
    *rest,
):
    summaries = rest[:device_count]
    in_ref, cot_ref, state_ref, adjoint_ref, grad_ref, everyone = rest[device_count:]
    lanes, rows, _ = fwd_re.shape
    states = lanes * LANES
    length = rows // CHUNKS
    whole = lambda ref, part: jnp.concatenate([ref[lane, part, :] for lane in range(lanes)], axis=1)
    for slot, summary in enumerate(summaries):
        everyone[slot] = summary[...]
    me = where_ref[0]
    gain = gain_of(decay_ref[...])
    f_re = jnp.zeros((1, states), jnp.float32)
    f_im, b_re, b_im = f_re, f_re, f_re
    for device in range(device_count - 1):
        entry = everyone[me ^ device]
        l_re, l_im, d_re, d_im = entry[0:1], entry[1:2], entry[2:3], entry[3:4]
        before = device < me
        f_re, f_im = (
            jnp.where(before, l_re * f_re - l_im * f_im + d_re, f_re),
            jnp.where(before, l_re * f_im + l_im * f_re + d_im, f_im),
        )
    for device in range(device_count - 1, 0, -1):
        entry = everyone[me ^ device]
        l_re, l_im, d_re, d_im = entry[0:1], entry[1:2], entry[4:5], entry[5:6]
        after = device > me
        b_re, b_im = (
            jnp.where(after, l_re * b_re + l_im * b_im + d_re, b_re),
            jnp.where(after, l_re * b_im - l_im * b_re + d_im, b_im),
        )
    for chunk in range(CHUNKS):
        part = pl.ds(chunk * length, length)
        a_re, a_im = whole(fwd_are, part), whole(fwd_aim, part)
        state_ref[part, pl.ds(0, states)] = (whole(fwd_re, part) + a_re * f_re - a_im * f_im).astype(
            jnp.bfloat16
        )
        state_ref[part, pl.ds(states, states)] = (
            whole(fwd_im, part) + a_re * f_im + a_im * f_re
        ).astype(jnp.bfloat16)
        l_re, l_im = chunk_ref[0, chunk : chunk + 1, :], chunk_ref[1, chunk : chunk + 1, :]
        f_re, f_im = (
            l_re * f_re - l_im * f_im + chunk_ref[2, chunk : chunk + 1, :],
            l_re * f_im + l_im * f_re + chunk_ref[3, chunk : chunk + 1, :],
        )
    for chunk in range(CHUNKS - 1, -1, -1):
        part = pl.ds(chunk * length, length)
        a_re, a_im = whole(back_are, part), whole(back_aim, part)
        adjoint_ref[part, pl.ds(0, states)] = (
            (whole(back_re, part) + a_re * b_re - a_im * b_im) * gain
        ).astype(jnp.bfloat16)
        adjoint_ref[part, pl.ds(states, states)] = (
            (whole(back_im, part) + a_re * b_im + a_im * b_re) * gain
        ).astype(jnp.bfloat16)
        l_re, l_im = chunk_ref[0, chunk : chunk + 1, :], chunk_ref[1, chunk : chunk + 1, :]
        b_re, b_im = (
            l_re * b_re + l_im * b_im + chunk_ref[4, chunk : chunk + 1, :],
            l_re * b_im - l_im * b_re + chunk_ref[5, chunk : chunk + 1, :],
        )
    over_rows = (((0,), (0,)), ((), ()))

    @pl.when(where_ref[1] == 0)
    def _():
        grad_ref[...] = lax.dot_general(
            cot_ref[...], state_ref[...], over_rows, preferred_element_type=jnp.float32
        )

    @pl.when(where_ref[1] != 0)
    def _():
        grad_ref[...] = lax.dot_general(
            in_ref[...], adjoint_ref[...], over_rows, preferred_element_type=jnp.float32
        )


def global_states(where, decay, chunk_totals, planes, summaries, flat_in, flat_cot):
    rows, width = flat_in.shape
    states = decay.shape[1]
    vmem = pl.BlockSpec(memory_space=pltpu.VMEM)
    return pl.pallas_call(
        functools.partial(states_kernel, len(summaries)),
        out_shape=[
            jax.ShapeDtypeStruct((rows, 2 * states), jnp.bfloat16),
            jax.ShapeDtypeStruct((rows, 2 * states), jnp.bfloat16),
            jax.ShapeDtypeStruct((width, 2 * states), jnp.float32),
        ],
        in_specs=[pl.BlockSpec(memory_space=pltpu.SMEM)] + [vmem] * (12 + len(summaries)),
        out_specs=[vmem] * 3,
        scratch_shapes=[pltpu.VMEM((len(summaries), 8, states), jnp.float32)],
        compiler_params=pltpu.CompilerParams(vmem_limit_bytes=VMEM_LIMIT),
        cost_estimate=pl.CostEstimate(
            flops=2 * rows * width * 2 * states, bytes_accessed=9 * 2**20, transcendentals=0
        ),
        name="global_states",
    )(where, decay, chunk_totals, *planes, *summaries, flat_in, flat_cot)


def own_grad_kernel(where_ref, in_ref, cot_ref, state_ref, adjoint_ref, grad_ref):
    over_rows = (((0,), (0,)), ((), ()))

    @pl.when(where_ref[1] == 0)
    def _():
        grad_ref[...] = lax.dot_general(
            in_ref[...], adjoint_ref[...], over_rows, preferred_element_type=jnp.float32
        )

    @pl.when(where_ref[1] != 0)
    def _():
        grad_ref[...] = lax.dot_general(
            cot_ref[...], state_ref[...], over_rows, preferred_element_type=jnp.float32
        )


def own_grad(where, flat_in, flat_cot, state_pairs, adjoint_pairs):
    rows, width = flat_in.shape
    vmem = pl.BlockSpec(memory_space=pltpu.VMEM)
    return pl.pallas_call(
        own_grad_kernel,
        out_shape=jax.ShapeDtypeStruct((width, state_pairs.shape[1]), jnp.float32),
        in_specs=[pl.BlockSpec(memory_space=pltpu.SMEM)] + [vmem] * 4,
        out_specs=vmem,
        compiler_params=pltpu.CompilerParams(vmem_limit_bytes=VMEM_LIMIT),
        cost_estimate=pl.CostEstimate(
            flops=2 * rows * width * state_pairs.shape[1],
            bytes_accessed=5 * 2**20,
            transcendentals=0,
        ),
        name="own_grad",
    )(where, flat_in, flat_cot, state_pairs, adjoint_pairs)


def mix_kernel(pair_ref, proj_ref, gain_ref, skip_ref, out_ref):
    mixed = lax.dot_general(
        pair_ref[...],
        proj_ref[...],
        (((1,), (1,)), ((), ())),
        preferred_element_type=jnp.float32,
    )
    out_ref[...] = (mixed + gain_ref[...] * skip_ref[...].astype(jnp.float32)).astype(jnp.bfloat16)


def mix(pairs, proj, skip_gain, skipped):
    rows, width = skipped.shape
    vmem = pl.BlockSpec(memory_space=pltpu.VMEM)
    return pl.pallas_call(
        mix_kernel,
        out_shape=jax.ShapeDtypeStruct(skipped.shape, jnp.bfloat16),
        in_specs=[vmem] * 4,
        out_specs=vmem,
        compiler_params=pltpu.CompilerParams(vmem_limit_bytes=VMEM_LIMIT),
        cost_estimate=pl.CostEstimate(
            flops=2 * rows * width * pairs.shape[1], bytes_accessed=4 * 2**20, transcendentals=0
        ),
        name="mix",
    )(pairs, proj, skip_gain, skipped)


def on_device(
    inputs, step_size, decay_rate, frequency, input_proj, output_proj, skip_gain, cotangent
):
    batch_count, row_count, model_width = inputs.shape
    state_count = decay_rate.shape[0]
    dp_count, context_count = lax.axis_size("dp"), lax.axis_size("context")
    dp_bits, context_bits = dp_count.bit_length() - 1, context_count.bit_length() - 1
    dp_place, context_place = lax.axis_index("dp"), lax.axis_index("context")
    core = dp_place & 1

    def swap(array, axis, bit):
        count = dp_count if axis == "dp" else context_count
        return lax.ppermute(array, axis, [(place, place ^ (1 << bit)) for place in range(count)])

    flat_in = inputs.reshape(row_count, model_width)
    flat_cot = cotangent.reshape(row_count, model_width)
    decay = decay_rate.reshape(1, state_count)
    where = jnp.stack([context_place, core]).astype(jnp.int32)
    *planes, chunk_totals, summary = local_scan(
        step_size.reshape(CHUNKS, row_count // CHUNKS),
        decay,
        frequency.reshape(1, state_count),
        flat_in,
        flat_cot,
        input_proj,
        output_proj,
    )
    summaries = [summary]
    for bit in range(context_bits):
        summaries = summaries + [swap(entry, "context", bit) for entry in summaries]
    state_pairs, adjoint_pairs, lent = global_states(
        where, decay, chunk_totals, planes, summaries, flat_in, flat_cot
    )
    borrowed = swap(lent, "dp", 0)
    kept = own_grad(where, flat_in, flat_cot, state_pairs, adjoint_pairs)
    outputs = mix(state_pairs, output_proj, skip_gain.reshape(1, model_width), flat_in)
    input_grad = mix(adjoint_pairs, input_proj, skip_gain.reshape(1, model_width), flat_cot)

    piece = model_width // (context_count * dp_count // 2)
    bits = [("context", bit) for bit in reversed(range(context_bits))]
    bits += [("dp", bit) for bit in reversed(range(1, dp_bits))]
    half = state_count
    shape = [2] * len(bits) + [piece, half]
    parts = [
        (kept[:, cols : cols + half].reshape(shape), borrowed[:, cols : cols + half].reshape(shape))
        for cols in (0, half)
    ]

    def side(axis, bit, mine):
        place = dp_place if axis == "dp" else context_place
        own = (place >> bit) & 1
        return own if mine else 1 - own

    def halve(pair, left, axis, bit):
        at = left.index((axis, bit))
        pick = lambda array, mine: lax.dynamic_index_in_dim(
            array, side(axis, bit, mine), at, keepdims=False
        )
        away = swap(pick(pair[0], False) + pick(pair[1], False), axis, bit)
        return (pick(pair[0], True) + pick(pair[1], True), away)

    dp_order = [("dp", bit) for bit in range(1, dp_bits)]
    orders = [dp_order + [("context", 0)], [("context", 0)] + dp_order]
    left = [list(bits), list(bits)]
    for steps in zip(*orders):
        for stream, step in enumerate(steps):
            parts[stream] = halve(parts[stream], left[stream], *step)
            left[stream].remove(step)
    kept = jnp.concatenate([parts[0][0], parts[1][0]], axis=-1)
    borrowed = jnp.concatenate([parts[0][1], parts[1][1]], axis=-1)
    pair, rest = (kept, borrowed), left[0]
    for bit in range(1, context_bits):
        pair = halve(pair, rest, "context", bit)
        rest.remove(("context", bit))
    grad_scale = float(batch_count * row_count * dp_count * context_count) ** (-0.5)
    share = (pair[0] + pair[1]) * grad_scale
    for bit in range(1, dp_bits):
        other = swap(share, "dp", bit)
        own_first = side("dp", bit, True) == 0
        share = jnp.where(
            own_first, jnp.concatenate([share, other]), jnp.concatenate([other, share])
        )
    other = swap(share, "dp", 0)
    return (
        outputs.reshape(inputs.shape),
        input_grad.reshape(inputs.shape),
        jnp.where(core == 0, share, other),
        jnp.where(core == 0, other, share),
    )


def solution(mesh):
    in_specs = (
        P("dp", "context", None),
        P("dp", "context"),
        P(),
        P(),
        P(),
        P(),
        P(),
        P("dp", "context", None),
    )
    out_specs = (
        P("dp", "context", None),
        P("dp", "context", None),
        P("context", None),
        P("context", None),
    )
    return jax.shard_map(
        on_device, mesh=mesh, in_specs=in_specs, out_specs=out_specs, check_vma=False
    )
```

```python
import functools

import jax
import jax.numpy as jnp
from jax import lax
from jax.experimental import pallas as pl
from jax.experimental.pallas import tpu as pltpu
from jax.sharding import PartitionSpec as P

CHUNKS = 8
LANES = 128
VMEM_LIMIT = 24 * 1024 * 1024
STREAMS = (((0, 1, "xyz"), (2, 3, "yxz")), ((1, 2, "xyz"), (3, 4, "yxz")))

TWO_OVER_PI = 0.6366197723675814
PIO2_HIGH = 1.5703125
PIO2_MID = 0.0004837512969970703
PIO2_LOW = 7.549789948768648e-08


def sin_cos(angle):
    quadrant_real = jnp.floor(angle * TWO_OVER_PI + 0.5)
    rest = angle - quadrant_real * PIO2_HIGH
    rest = rest - quadrant_real * PIO2_MID
    rest = rest - quadrant_real * PIO2_LOW
    square = rest * rest
    sine = rest + rest * square * (
        -1.6666654611e-1 + square * (8.3321608736e-3 + square * -1.9515295891e-4)
    )
    cosine = (
        1.0
        - 0.5 * square
        + square
        * square
        * (4.166664568298827e-2 + square * (-1.388731625493765e-3 + square * 2.443315711809948e-5))
    )
    quadrant = quadrant_real.astype(jnp.int32)
    swapped = (quadrant & 1) == 1
    sin_base = jnp.where(swapped, cosine, sine)
    cos_base = jnp.where(swapped, sine, cosine)
    sin_value = jnp.where((quadrant & 2) == 2, -sin_base, sin_base)
    cos_value = jnp.where(((quadrant + 1) & 2) == 2, -cos_base, cos_base)
    return sin_value, cos_value


def gain_of(decay):
    twice = 2.0 * decay
    series = 1.0 / 3628800.0
    for factorial in (362880.0, 40320.0, 5040.0, 720.0, 120.0, 24.0, 6.0, 2.0, 1.0):
        series = 1.0 / factorial - twice * series
    return jnp.sqrt(jnp.where(twice < 0.5, twice * series, 1.0 - jnp.exp(-twice)))


def places():
    return lax.axis_index("context"), lax.axis_index("dp")


def local_scan_kernel(
    step_hbm,
    decay_hbm,
    frequency_hbm,
    in_hbm,
    cot_hbm,
    in_proj_hbm,
    out_proj_hbm,
    fwd_re,
    fwd_im,
    fwd_are,
    fwd_aim,
    back_re,
    back_im,
    back_are,
    back_aim,
    chunk_ref,
    summary_ref,
    outside_ref,
    in_vmem,
    cot_vmem,
    in_proj_vmem,
    out_proj_vmem,
    decay_ref,
    step_ref,
    frequency_ref,
    lam_re,
    lam_im,
    drive,
    adjoint,
    sems,
):
    rows = in_vmem.shape[0]
    length = rows // CHUNKS
    states = decay_ref.shape[1]
    lanes = states // LANES
    copies = [
        pltpu.make_async_copy(source, target, sems.at[slot])
        for slot, (source, target) in enumerate(
            (
                (step_hbm, step_ref),
                (decay_hbm, decay_ref),
                (frequency_hbm, frequency_ref),
                (in_hbm, in_vmem),
                (in_proj_hbm, in_proj_vmem),
                (cot_hbm, cot_vmem),
                (out_proj_hbm, out_proj_vmem),
            )
        )
    ]
    for copy in copies:
        copy.start()
    for copy in copies[:3]:
        copy.wait()
    loads = copies[3:]
    decay = decay_ref[...]
    frequency = frequency_ref[...]
    gain = gain_of(decay)
    steps = jnp.concatenate(
        [step_ref[:, chunk * length : (chunk + 1) * length] for chunk in range(CHUNKS)], axis=0
    )
    for place in range(length):
        here = jnp.broadcast_to(steps[:, place : place + 1], (CHUNKS, states))
        damping = jnp.exp(-here * decay)
        sine, cosine = sin_cos(here * frequency)
        lam_re[pl.ds(place * CHUNKS, CHUNKS), :] = damping * cosine
        lam_im[pl.ds(place * CHUNKS, CHUNKS), :] = damping * sine
    loads[0].wait()
    loads[1].wait()
    pair_gain = jnp.concatenate([gain, gain], axis=1)
    driven = (
        jnp.dot(in_vmem[...], in_proj_vmem[...], preferred_element_type=jnp.float32) * pair_gain
    )
    for lane in range(2 * lanes):
        drive[lane] = driven[:, lane * LANES : (lane + 1) * LANES]
    loads[2].wait()
    loads[3].wait()
    driven = jnp.dot(cot_vmem[...], out_proj_vmem[...], preferred_element_type=jnp.float32)
    for lane in range(2 * lanes):
        adjoint[lane] = driven[:, lane * LANES : (lane + 1) * LANES]

    def gather(ref, first, spread):
        return jnp.concatenate([ref[first + lane, spread, :] for lane in range(lanes)], axis=1)

    def scatter(ref, spread, value):
        for lane in range(lanes):
            ref[lane, spread, :] = value[:, lane * LANES : (lane + 1) * LANES]

    def body(place, carry):
        f_are, f_aim, f_re, f_im, b_are, b_aim, b_re, b_im = carry
        tile = pl.ds(pl.multiple_of(place * CHUNKS, CHUNKS), CHUNKS)
        spread = pl.ds(place, CHUNKS, stride=length)
        l_re, l_im = lam_re[tile, :], lam_im[tile, :]
        new_are = l_re * f_are - l_im * f_aim
        new_aim = l_re * f_aim + l_im * f_are
        new_re = l_re * f_re - l_im * f_im + gather(drive, 0, spread)
        new_im = l_re * f_im + l_im * f_re + gather(drive, lanes, spread)
        scatter(fwd_are, spread, new_are)
        scatter(fwd_aim, spread, new_aim)
        scatter(fwd_re, spread, new_re)
        scatter(fwd_im, spread, new_im)
        mirror = length - 1 - place
        tile = pl.ds(pl.multiple_of(mirror * CHUNKS, CHUNKS), CHUNKS)
        spread = pl.ds(mirror, CHUNKS, stride=length)
        l_re, l_im = lam_re[tile, :], lam_im[tile, :]
        a_re = b_re + gather(adjoint, 0, spread)
        a_im = b_im + gather(adjoint, lanes, spread)
        scatter(back_are, spread, b_are)
        scatter(back_aim, spread, b_aim)
        scatter(back_re, spread, a_re)
        scatter(back_im, spread, a_im)
        next_are = l_re * b_are + l_im * b_aim
        next_aim = l_re * b_aim - l_im * b_are
        next_re = l_re * a_re + l_im * a_im
        next_im = l_re * a_im - l_im * a_re
        return (new_are, new_aim, new_re, new_im, next_are, next_aim, next_re, next_im)

    zero = jnp.zeros((CHUNKS, states), jnp.float32)
    one = jnp.ones((CHUNKS, states), jnp.float32)
    totals = lax.fori_loop(
        0, length, body, (one, zero, zero, zero, one, zero, zero, zero), unroll=4
    )
    a_re, a_im, f_re, f_im, _, _, b_re, b_im = totals
    for slot, part in enumerate((a_re, a_im, f_re, f_im, b_re, b_im)):
        chunk_ref[slot] = part
    row = lambda part, chunk: part[chunk : chunk + 1, :]
    t_are, t_aim = row(a_re, 0), row(a_im, 0)
    t_re, t_im = row(f_re, 0), row(f_im, 0)
    for chunk in range(1, CHUNKS):
        l_re, l_im = row(a_re, chunk), row(a_im, chunk)
        t_are, t_aim = l_re * t_are - l_im * t_aim, l_re * t_aim + l_im * t_are
        t_re, t_im = (
            l_re * t_re - l_im * t_im + row(f_re, chunk),
            l_re * t_im + l_im * t_re + row(f_im, chunk),
        )
    u_re, u_im = row(b_re, CHUNKS - 1), row(b_im, CHUNKS - 1)
    for chunk in range(CHUNKS - 2, -1, -1):
        l_re, l_im = row(a_re, chunk), row(a_im, chunk)
        u_re, u_im = (
            l_re * u_re + l_im * u_im + row(b_re, chunk),
            l_re * u_im - l_im * u_re + row(b_im, chunk),
        )
    summary_ref[...] = jnp.concatenate(
        [t_are, t_aim, t_re, t_im, u_re, u_im, t_are, t_aim], axis=0
    )
    one, zero = jnp.ones_like(t_are), jnp.zeros_like(t_are)
    outside_ref[...] = jnp.concatenate([one, zero, zero, zero] * 2, axis=0)


def held(shape, dtype=jnp.float32):
    return pltpu.VMEM(shape, dtype)


def call(kernel, name, out_shape, *args, inputs=None, outputs=None, scratch=(), flops=0):
    vmem = pl.BlockSpec(memory_space=pltpu.VMEM)
    return pl.pallas_call(
        kernel,
        out_shape=out_shape,
        in_specs=inputs or [vmem] * len(args),
        out_specs=outputs or jax.tree.map(lambda _: vmem, out_shape),
        scratch_shapes=scratch,
        compiler_params=pltpu.CompilerParams(vmem_limit_bytes=VMEM_LIMIT),
        cost_estimate=pl.CostEstimate(
            flops=flops, bytes_accessed=max(flops // 1000, 1024), transcendentals=0
        ),
        name=name,
    )(*args)


def local_scan(step_row, decay, frequency, flat_in, flat_cot, input_proj, output_proj):
    rows = flat_in.shape[0]
    states = decay.shape[1]
    lanes = states // LANES
    args = [
        pltpu.with_memory_space_constraint(array, pltpu.HBM)
        for array in (step_row, decay, frequency, flat_in, flat_cot, input_proj, output_proj)
    ]
    return call(
        local_scan_kernel,
        "local_scan",
        [held((lanes, rows, LANES))] * 8
        + [held((6, CHUNKS, states)), held((8, states)), held((8, states))]
        + [held(array.shape, array.dtype) for array in args[3:]]
        + [held(decay.shape)],
        *args,
        inputs=[pl.BlockSpec(memory_space=pltpu.HBM)] * 7,
        scratch=[
            pltpu.VMEM(step_row.shape, jnp.float32),
            pltpu.VMEM(frequency.shape, jnp.float32),
            pltpu.VMEM((rows, states), jnp.float32),
            pltpu.VMEM((rows, states), jnp.float32),
            pltpu.VMEM((2 * lanes, rows, LANES), jnp.float32),
            pltpu.VMEM((2 * lanes, rows, LANES), jnp.float32),
            pltpu.SemaphoreType.DMA((7,)),
        ],
        flops=4 * rows * flat_in.shape[1] * 2 * states,
    )


def times(a, b):
    return a[0] * b[0] - a[1] * b[1], a[0] * b[1] + a[1] * b[0]


def times_conj(a, b):
    return a[0] * b[0] + a[1] * b[1], a[0] * b[1] - a[1] * b[0]


def plus(a, b):
    return a[0] + b[0], a[1] + b[1]


def pick(upper, a, b):
    return tuple(jnp.where(upper, x, y) for x, y in zip(a, b))


def pairs_of(array):
    return [(array[row : row + 1], array[row + 1 : row + 2]) for row in range(0, 8, 2)]


def widen(bit, outside, other):
    upper = ((lax.axis_index("context") >> bit) & 1) == 1
    below, below_sum, above, above_sum = outside
    product, forward, backward, _ = other
    return (
        pick(upper, times(below, product), below),
        pick(upper, plus(times(below, forward), below_sum), below_sum),
        pick(upper, above, times(above, product)),
        pick(upper, above_sum, plus(times_conj(above, backward), above_sum)),
    )


def combine_kernel(bit, total_ref, outside_ref, other_ref, total_out, outside_out):
    other = pairs_of(other_ref[...])
    mine = pairs_of(total_ref[...])
    outside = widen(bit, pairs_of(outside_ref[...]), other)
    outside_out[...] = jnp.concatenate([part for pair in outside for part in pair], axis=0)
    upper = ((lax.axis_index("context") >> bit) & 1) == 1
    low = [pick(upper, theirs, ours) for theirs, ours in zip(other, mine)]
    high = [pick(upper, ours, theirs) for theirs, ours in zip(other, mine)]
    product = times(low[0], high[0])
    forward = plus(times(high[0], low[1]), high[1])
    backward = plus(times_conj(low[0], high[2]), low[2])
    total_out[...] = jnp.concatenate([*product, *forward, *backward, *product], axis=0)


def states_kernel(
    bit,
    decay_ref,
    chunk_ref,
    fwd_re,
    fwd_im,
    fwd_are,
    fwd_aim,
    back_re,
    back_im,
    back_are,
    back_aim,
    outside_ref,
    other_ref,
    in_ref,
    cot_ref,
    state_ref,
    adjoint_ref,
    grad_ref,
):
    lanes, rows, _ = fwd_re.shape
    states = lanes * LANES
    length = rows // CHUNKS
    whole = lambda ref, part: jnp.concatenate([ref[lane, part, :] for lane in range(lanes)], axis=1)
    dp_place = places()[1]
    gain = gain_of(decay_ref[...])
    outside = widen(bit, pairs_of(outside_ref[...]), pairs_of(other_ref[...]))
    (f_re, f_im), (b_re, b_im) = outside[1], outside[3]
    for chunk in range(CHUNKS):
        part = pl.ds(chunk * length, length)
        a_re, a_im = whole(fwd_are, part), whole(fwd_aim, part)
        state_ref[part, pl.ds(0, states)] = (whole(fwd_re, part) + a_re * f_re - a_im * f_im).astype(
            jnp.bfloat16
        )
        state_ref[part, pl.ds(states, states)] = (
            whole(fwd_im, part) + a_re * f_im + a_im * f_re
        ).astype(jnp.bfloat16)
        l_re, l_im = chunk_ref[0, chunk : chunk + 1, :], chunk_ref[1, chunk : chunk + 1, :]
        f_re, f_im = (
            l_re * f_re - l_im * f_im + chunk_ref[2, chunk : chunk + 1, :],
            l_re * f_im + l_im * f_re + chunk_ref[3, chunk : chunk + 1, :],
        )
    for chunk in range(CHUNKS - 1, -1, -1):
        part = pl.ds(chunk * length, length)
        a_re, a_im = whole(back_are, part), whole(back_aim, part)
        adjoint_ref[part, pl.ds(0, states)] = (
            (whole(back_re, part) + a_re * b_re - a_im * b_im) * gain
        ).astype(jnp.bfloat16)
        adjoint_ref[part, pl.ds(states, states)] = (
            (whole(back_im, part) + a_re * b_im + a_im * b_re) * gain
        ).astype(jnp.bfloat16)
        l_re, l_im = chunk_ref[0, chunk : chunk + 1, :], chunk_ref[1, chunk : chunk + 1, :]
        b_re, b_im = (
            l_re * b_re + l_im * b_im + chunk_ref[4, chunk : chunk + 1, :],
            l_re * b_im - l_im * b_re + chunk_ref[5, chunk : chunk + 1, :],
        )
    over_rows = (((0,), (0,)), ((), ()))

    @pl.when(dp_place & 1 == 0)
    def _():
        grad_ref[...] = lax.dot_general(
            cot_ref[...], state_ref[...], over_rows, preferred_element_type=jnp.float32
        )

    @pl.when(dp_place & 1 == 1)
    def _():
        grad_ref[...] = lax.dot_general(
            in_ref[...], adjoint_ref[...], over_rows, preferred_element_type=jnp.float32
        )


def global_states(bit, decay, chunk_totals, planes, outside, other, flat_in, flat_cot):
    rows, width = flat_in.shape
    states = decay.shape[1]
    return call(
        functools.partial(states_kernel, bit),
        "global_states",
        [
            held((rows, 2 * states), jnp.bfloat16),
            held((rows, 2 * states), jnp.bfloat16),
            held((width, 2 * states)),
        ],
        decay,
        chunk_totals,
        *planes,
        outside,
        other,
        flat_in,
        flat_cot,
        flops=2 * rows * width * 2 * states,
    )


def products_kernel(
    in_ref,
    cot_ref,
    state_ref,
    adjoint_ref,
    in_proj_ref,
    out_proj_ref,
    skip_ref,
    grad_ref,
    out_hbm,
    back_hbm,
    out_ref,
    back_ref,
    sems,
):
    over_rows = (((0,), (0,)), ((), ()))
    over_states = (((1,), (1,)), ((), ()))
    skip = skip_ref[...]
    stores = []
    for slot, (pairs, proj, skipped, target, result) in enumerate(
        (
            (state_ref, out_proj_ref, in_ref, out_ref, out_hbm),
            (adjoint_ref, in_proj_ref, cot_ref, back_ref, back_hbm),
        )
    ):
        mixed = lax.dot_general(
            pairs[...], proj[...], over_states, preferred_element_type=jnp.float32
        )
        target[...] = (mixed + skip * skipped[...].astype(jnp.float32)).astype(jnp.bfloat16)
        stores.append(pltpu.make_async_copy(target, result, sems.at[slot]))
        stores[-1].start()
    core = places()[1] & 1

    @pl.when(core == 0)
    def _():
        grad_ref[...] = lax.dot_general(
            in_ref[...], adjoint_ref[...], over_rows, preferred_element_type=jnp.float32
        )

    @pl.when(core == 1)
    def _():
        grad_ref[...] = lax.dot_general(
            cot_ref[...], state_ref[...], over_rows, preferred_element_type=jnp.float32
        )

    for store in stores:
        store.wait()


def products(flat_in, flat_cot, state_pairs, adjoint_pairs, input_proj, output_proj, skip_gain):
    rows, width = flat_in.shape
    vmem = pl.BlockSpec(memory_space=pltpu.VMEM)
    hbm = pl.BlockSpec(memory_space=pltpu.HBM)
    return call(
        products_kernel,
        "products",
        [
            held((width, state_pairs.shape[1])),
            jax.ShapeDtypeStruct(flat_in.shape, jnp.bfloat16),
            jax.ShapeDtypeStruct(flat_in.shape, jnp.bfloat16),
        ],
        flat_in,
        flat_cot,
        state_pairs,
        adjoint_pairs,
        input_proj,
        output_proj,
        skip_gain,
        outputs=[vmem, hbm, hbm],
        scratch=[
            pltpu.VMEM(flat_in.shape, jnp.bfloat16),
            pltpu.VMEM(flat_in.shape, jnp.bfloat16),
            pltpu.SemaphoreType.DMA((2,)),
        ],
        flops=6 * rows * width * state_pairs.shape[1],
    )


def own_bit(step):
    axis, bit = step
    return (lax.axis_index(axis) >> bit) & 1


def add_kernel(plans, scale, *refs):
    merged = plans[0][3] is None
    count = 1 if merged else len(plans)
    outs = refs[len(refs) - count :]
    at = 0
    for number, (layouts, columns, settled, sent) in enumerate(plans):
        out = outs[0] if merged else outs[number]
        sources = refs[at : at + len(layouts)]
        at += len(layouts)
        free = [step for step in layouts[-1] if step not in settled and step != sent]
        fixed = {step: own_bit(step) for step in settled}
        if sent is not None:
            fixed[sent] = 1 - own_bit(sent)
        for block in range(2 ** len(free)):
            values = dict(fixed)
            for place, step in enumerate(free):
                values[step] = (block >> (len(free) - 1 - place)) & 1
            total = None
            for source, layout in zip(sources, layouts):
                index = 0
                for step in layout:
                    index = index * 2 + values[step]
                wide = source.shape[2] != columns[1] - columns[0]
                part = source[index, :, columns[0] : columns[1]] if wide else source[index]
                total = part if total is None else total + part
            if merged:
                out[block, :, columns[0] : columns[1]] = total * scale
            else:
                out[block] = total


def gather_kernel(*refs):
    in_ref, out_ref = refs[-2:]
    dp_place = places()[1]
    for offset, share in enumerate(refs[:-2]):
        place = dp_place ^ offset

        @pl.when(place & 1 == 0)
        def _():
            in_ref[place >> 1] = share[0]

        @pl.when(place & 1 == 1)
        def _():
            out_ref[place >> 1] = share[0]


def on_device(
    inputs, step_size, decay_rate, frequency, input_proj, output_proj, skip_gain, cotangent
):
    batch_count, row_count, model_width = inputs.shape
    state_count = decay_rate.shape[0]
    dp_count, context_count = lax.axis_size("dp"), lax.axis_size("context")
    dp_bits, context_bits = dp_count.bit_length() - 1, context_count.bit_length() - 1

    def swap(array, step):
        axis, bit = step
        count = dp_count if axis == "dp" else context_count
        return lax.ppermute(array, axis, [(place, place ^ (1 << bit)) for place in range(count)])

    *planes, chunk_totals, total, outside, flat_in, flat_cot, in_proj, out_proj, decay = local_scan(
        step_size,
        decay_rate.reshape(1, state_count),
        frequency.reshape(1, state_count),
        inputs.reshape(row_count, model_width),
        cotangent.reshape(row_count, model_width),
        input_proj,
        output_proj,
    )
    for bit in range(context_bits - 1):
        other = swap(total, ("context", bit))
        total, outside = call(
            functools.partial(combine_kernel, bit),
            "combine",
            [held(total.shape), held(outside.shape)],
            total,
            outside,
            other,
        )
    last = context_bits - 1
    state_pairs, adjoint_pairs, lent = global_states(
        last, decay, chunk_totals, planes, outside, swap(total, ("context", last)), flat_in, flat_cot
    )
    borrowed = swap(lent, ("dp", 0))
    kept, outputs, input_grad = products(
        flat_in,
        flat_cot,
        state_pairs,
        adjoint_pairs,
        in_proj,
        out_proj,
        skip_gain.reshape(1, model_width),
    )

    extra_bits = [("dp", bit) for bit in range(1, dp_bits)]
    piece = model_width // (context_count * dp_count // 2)
    layout = [("context", bit) for bit in reversed(range(context_bits))] + extra_bits[::-1]
    blocks = (2 ** len(layout), piece, 2 * state_count)
    grad_scale = float(batch_count * row_count * dp_count * context_count) ** (-0.5)
    z_bits = [("context", bit) for bit in range(1, context_bits)]
    y_bits = [("context", 0)]
    by_name = {"x": extra_bits, "y": y_bits, "z": z_bits, "Z": z_bits[::-1]}
    groups = []
    for plan in STREAMS:
        groups.append([])
        for first, past, names in plan:
            groups[-1].append(
                {
                    "columns": (first * LANES, past * LANES),
                    "sources": [kept.reshape(blocks), borrowed.reshape(blocks)],
                    "layouts": [layout, layout],
                    "settled": [],
                    "order": [step for name in names for step in by_name[name]],
                }
            )
    streams = [stream for group in groups for stream in group]

    def add(streams, steps, scale=None):
        plans, args, shapes = [], [], []
        for stream, step in zip(streams, steps):
            plans.append((stream["layouts"], stream["columns"], list(stream["settled"]), step))
            args += stream["sources"]
            free = len(layout) - len(stream["settled"]) - (step is not None)
            width = stream["columns"][1] - stream["columns"][0]
            shapes.append(held((2**free, piece, width)))
        if scale is not None:
            shapes = [held((1, piece, 2 * state_count))]
        name = "halve" if scale is None else "share"
        return call(functools.partial(add_kernel, plans, scale), name, shapes, *args)

    for place in range(len(layout)):
        for group in groups:
            steps = [stream["order"][place] for stream in group]
            for stream, step, away in zip(group, steps, add(group, steps)):
                stream["settled"] = stream["settled"] + [step]
                left = [bit for bit in layout if bit not in stream["settled"]]
                stream["sources"] = stream["sources"] + [swap(away, step)]
                stream["layouts"] = stream["layouts"] + [left]
    shares = list(add(streams, [None] * len(streams), grad_scale))
    for bit in [*range(1, dp_bits), 0]:
        shares = shares + [swap(share, ("dp", bit)) for share in shares]
    order = [0]
    for bit in [*range(1, dp_bits), 0]:
        order = order + [offset ^ (1 << bit) for offset in order]
    by_offset = [shares[order.index(offset)] for offset in range(dp_count)]
    whole = jax.ShapeDtypeStruct((dp_count // 2, piece, 2 * state_count), jnp.float32)
    grads = call(gather_kernel, "gather", [whole, whole], *by_offset)
    grads = [grad.reshape(model_width // context_count, 2 * state_count) for grad in grads]
    return (outputs.reshape(inputs.shape), input_grad.reshape(inputs.shape), *grads)


def solution(mesh):
    in_specs = (
        P("dp", "context", None),
        P("dp", "context"),
        P(),
        P(),
        P(),
        P(),
        P(),
        P("dp", "context", None),
    )
    out_specs = (
        P("dp", "context", None),
        P("dp", "context", None),
        P("context", None),
        P("context", None),
    )
    return jax.shard_map(
        on_device, mesh=mesh, in_specs=in_specs, out_specs=out_specs, check_vma=False
    )
```

```python
import functools

import jax
import jax.numpy as jnp
from jax import lax
from jax.experimental import pallas as pl
from jax.experimental.pallas import tpu as pltpu
from jax.sharding import PartitionSpec as P

CHUNKS = 8
LANES = 128
GROUP = 256
VMEM_LIMIT = 24 * 1024 * 1024
STREAMS = ((0, 2, "xyz", "yzx"), (2, 4, "xyz", "yzx"))

TWO_OVER_PI = 0.6366197723675814
PIO2_HIGH = 1.5703125
PIO2_MID = 0.0004837512969970703
PIO2_LOW = 7.549789948768648e-08


def sin_cos(angle):
    quadrant_real = jnp.floor(angle * TWO_OVER_PI + 0.5)
    rest = angle - quadrant_real * PIO2_HIGH
    rest = rest - quadrant_real * PIO2_MID
    rest = rest - quadrant_real * PIO2_LOW
    square = rest * rest
    sine = rest + rest * square * (
        -1.6666654611e-1 + square * (8.3321608736e-3 + square * -1.9515295891e-4)
    )
    cosine = (
        1.0
        - 0.5 * square
        + square
        * square
        * (4.166664568298827e-2 + square * (-1.388731625493765e-3 + square * 2.443315711809948e-5))
    )
    quadrant = quadrant_real.astype(jnp.int32)
    swapped = (quadrant & 1) == 1
    sin_base = jnp.where(swapped, cosine, sine)
    cos_base = jnp.where(swapped, sine, cosine)
    sin_value = jnp.where((quadrant & 2) == 2, -sin_base, sin_base)
    cos_value = jnp.where(((quadrant + 1) & 2) == 2, -cos_base, cos_base)
    return sin_value, cos_value


def gain_of(decay):
    twice = 2.0 * decay
    series = 1.0 / 3628800.0
    for factorial in (362880.0, 40320.0, 5040.0, 720.0, 120.0, 24.0, 6.0, 2.0, 1.0):
        series = 1.0 / factorial - twice * series
    return jnp.sqrt(jnp.where(twice < 0.5, twice * series, 1.0 - jnp.exp(-twice)))


def places():
    return lax.axis_index("context"), lax.axis_index("dp")


def shuffle(back=False):
    length = GROUP // CHUNKS
    scan = lax.broadcasted_iota(jnp.int32, (GROUP, GROUP), 1 if back else 0)
    time = lax.broadcasted_iota(jnp.int32, (GROUP, GROUP), 0 if back else 1)
    return jnp.where(time == (scan % CHUNKS) * length + scan // CHUNKS, 1.0, 0.0).astype(
        jnp.bfloat16
    )


def local_scan_kernel(
    step_hbm,
    decay_hbm,
    frequency_hbm,
    in_hbm,
    cot_hbm,
    in_proj_hbm,
    out_proj_hbm,
    fwd_re,
    fwd_im,
    fwd_are,
    fwd_aim,
    back_re,
    back_im,
    back_are,
    back_aim,
    chunk_ref,
    summary_ref,
    outside_ref,
    in_vmem,
    cot_vmem,
    in_proj_vmem,
    out_proj_vmem,
    decay_ref,
    step_ref,
    frequency_ref,
    in_time,
    cot_time,
    lam_re,
    lam_im,
    drive,
    adjoint,
    sems,
):
    rows = in_vmem.shape[0]
    groups = rows // GROUP
    length = GROUP // CHUNKS
    states = decay_ref.shape[1]
    copies = [
        pltpu.make_async_copy(source, target, sems.at[slot])
        for slot, (source, target) in enumerate(
            (
                (step_hbm, step_ref),
                (decay_hbm, decay_ref),
                (frequency_hbm, frequency_ref),
                (in_hbm, in_time),
                (in_proj_hbm, in_proj_vmem),
                (cot_hbm, cot_time),
                (out_proj_hbm, out_proj_vmem),
            )
        )
    ]
    for copy in copies:
        copy.start()
    for copy in copies[:3]:
        copy.wait()
    loads = copies[3:]
    decay = decay_ref[...]
    frequency = frequency_ref[...]
    gain = gain_of(decay)
    steps = [
        jnp.concatenate(
            [
                step_ref[:, first : first + length]
                for first in range(group * GROUP, (group + 1) * GROUP, length)
            ],
            axis=0,
        )
        for group in range(groups)
    ]
    for place in range(length):
        for group in range(groups):
            here = jnp.broadcast_to(steps[group][:, place : place + 1], (CHUNKS, states))
            damping = jnp.exp(-here * decay)
            sine, cosine = sin_cos(here * frequency)
            tile = pl.ds(group * GROUP + place * CHUNKS, CHUNKS)
            lam_re[tile, :] = damping * cosine
            lam_im[tile, :] = damping * sine
    to_scan = shuffle()
    pair_gain = jnp.concatenate([gain, gain], axis=1)
    for load, time_ref, scan_ref, proj_ref, target in (
        (loads[:2], in_time, in_vmem, in_proj_vmem, drive),
        (loads[2:], cot_time, cot_vmem, out_proj_vmem, adjoint),
    ):
        load[0].wait()
        for group in range(groups):
            part = pl.ds(group * GROUP, GROUP)
            scan_ref[part, :] = jnp.dot(
                to_scan, time_ref[part, :], preferred_element_type=jnp.float32
            ).astype(jnp.bfloat16)
        load[1].wait()
        driven = jnp.dot(scan_ref[...], proj_ref[...], preferred_element_type=jnp.float32)
        target[...] = driven * pair_gain if target is drive else driven
    re_cols, im_cols = pl.ds(0, states), pl.ds(states, states)

    def body(place, carry):
        results = []
        for group in range(groups):
            f_are, f_aim, f_re, f_im, b_are, b_aim, b_re, b_im = carry[8 * group : 8 * group + 8]
            first = group * GROUP + place * CHUNKS
            tile = pl.ds(pl.multiple_of(first, CHUNKS), CHUNKS)
            l_re, l_im = lam_re[tile, :], lam_im[tile, :]
            new_are = l_re * f_are - l_im * f_aim
            new_aim = l_re * f_aim + l_im * f_are
            new_re = l_re * f_re - l_im * f_im + drive[tile, re_cols]
            new_im = l_re * f_im + l_im * f_re + drive[tile, im_cols]
            fwd_are[tile, :] = new_are
            fwd_aim[tile, :] = new_aim
            fwd_re[tile, :] = new_re
            fwd_im[tile, :] = new_im
            first = group * GROUP + (length - 1 - place) * CHUNKS
            tile = pl.ds(pl.multiple_of(first, CHUNKS), CHUNKS)
            l_re, l_im = lam_re[tile, :], lam_im[tile, :]
            a_re = b_re + adjoint[tile, re_cols]
            a_im = b_im + adjoint[tile, im_cols]
            back_are[tile, :] = b_are
            back_aim[tile, :] = b_aim
            back_re[tile, :] = a_re
            back_im[tile, :] = a_im
            results += [
                new_are,
                new_aim,
                new_re,
                new_im,
                l_re * b_are + l_im * b_aim,
                l_re * b_aim - l_im * b_are,
                l_re * a_re + l_im * a_im,
                l_re * a_im - l_im * a_re,
            ]
        return tuple(results)

    zero = jnp.zeros((CHUNKS, states), jnp.float32)
    one = jnp.ones((CHUNKS, states), jnp.float32)
    totals = lax.fori_loop(
        0, length, body, (one, zero, zero, zero, one, zero, zero, zero) * groups, unroll=4
    )
    parts = [
        [totals[8 * group + slot] for slot in (0, 1, 2, 3, 6, 7)] for group in range(groups)
    ]
    for group in range(groups):
        for slot, part in enumerate(parts[group]):
            chunk_ref[slot, pl.ds(group * CHUNKS, CHUNKS), :] = part
    rows_of = [
        [part[chunk : chunk + 1, :] for part in parts[group]]
        for group in range(groups)
        for chunk in range(CHUNKS)
    ]
    t_are, t_aim, t_re, t_im = rows_of[0][:4]
    for l_re, l_im, d_re, d_im, _, _ in rows_of[1:]:
        t_are, t_aim = l_re * t_are - l_im * t_aim, l_re * t_aim + l_im * t_are
        t_re, t_im = l_re * t_re - l_im * t_im + d_re, l_re * t_im + l_im * t_re + d_im
    u_re, u_im = rows_of[-1][4:]
    for l_re, l_im, _, _, d_re, d_im in rows_of[-2::-1]:
        u_re, u_im = l_re * u_re + l_im * u_im + d_re, l_re * u_im - l_im * u_re + d_im
    summary_ref[...] = jnp.concatenate(
        [t_are, t_aim, t_re, t_im, u_re, u_im, t_are, t_aim], axis=0
    )
    one, zero = jnp.ones_like(t_are), jnp.zeros_like(t_are)
    outside_ref[...] = jnp.concatenate([one, zero, zero, zero] * 2, axis=0)


def held(shape, dtype=jnp.float32):
    return pltpu.VMEM(shape, dtype)


def call(kernel, name, out_shape, *args, inputs=None, outputs=None, scratch=(), flops=0):
    vmem = pl.BlockSpec(memory_space=pltpu.VMEM)
    return pl.pallas_call(
        kernel,
        out_shape=out_shape,
        in_specs=inputs or [vmem] * len(args),
        out_specs=outputs or jax.tree.map(lambda _: vmem, out_shape),
        scratch_shapes=scratch,
        compiler_params=pltpu.CompilerParams(vmem_limit_bytes=VMEM_LIMIT),
        cost_estimate=pl.CostEstimate(
            flops=flops, bytes_accessed=max(flops // 1000, 1024), transcendentals=0
        ),
        name=name,
    )(*args)


def local_scan(step_row, decay, frequency, flat_in, flat_cot, input_proj, output_proj):
    rows = flat_in.shape[0]
    states = decay.shape[1]
    args = [
        pltpu.with_memory_space_constraint(array, pltpu.HBM)
        for array in (step_row, decay, frequency, flat_in, flat_cot, input_proj, output_proj)
    ]
    return call(
        local_scan_kernel,
        "local_scan",
        [held((rows, states))] * 8
        + [held((6, rows // GROUP * CHUNKS, states)), held((8, states)), held((8, states))]
        + [held(array.shape, array.dtype) for array in args[3:]]
        + [held(decay.shape)],
        *args,
        inputs=[pl.BlockSpec(memory_space=pltpu.HBM)] * 7,
        scratch=[
            pltpu.VMEM(step_row.shape, jnp.float32),
            pltpu.VMEM(frequency.shape, jnp.float32),
            pltpu.VMEM(flat_in.shape, flat_in.dtype),
            pltpu.VMEM(flat_cot.shape, flat_cot.dtype),
            pltpu.VMEM((rows, states), jnp.float32),
            pltpu.VMEM((rows, states), jnp.float32),
            pltpu.VMEM((rows, 2 * states), jnp.float32),
            pltpu.VMEM((rows, 2 * states), jnp.float32),
            pltpu.SemaphoreType.DMA((7,)),
        ],
        flops=4 * rows * flat_in.shape[1] * 2 * states,
    )


def times(a, b):
    return a[0] * b[0] - a[1] * b[1], a[0] * b[1] + a[1] * b[0]


def times_conj(a, b):
    return a[0] * b[0] + a[1] * b[1], a[0] * b[1] - a[1] * b[0]


def plus(a, b):
    return a[0] + b[0], a[1] + b[1]


def pick(upper, a, b):
    return tuple(jnp.where(upper, x, y) for x, y in zip(a, b))


def pairs_of(array):
    return [(array[row : row + 1], array[row + 1 : row + 2]) for row in range(0, 8, 2)]


def widen(bit, outside, other):
    upper = ((lax.axis_index("context") >> bit) & 1) == 1
    below, below_sum, above, above_sum = outside
    product, forward, backward, _ = other
    return (
        pick(upper, times(below, product), below),
        pick(upper, plus(times(below, forward), below_sum), below_sum),
        pick(upper, above, times(above, product)),
        pick(upper, above_sum, plus(times_conj(above, backward), above_sum)),
    )


def combine_kernel(bit, total_ref, outside_ref, other_ref, total_out, outside_out):
    other = pairs_of(other_ref[...])
    mine = pairs_of(total_ref[...])
    outside = widen(bit, pairs_of(outside_ref[...]), other)
    outside_out[...] = jnp.concatenate([part for pair in outside for part in pair], axis=0)
    upper = ((lax.axis_index("context") >> bit) & 1) == 1
    low = [pick(upper, theirs, ours) for theirs, ours in zip(other, mine)]
    high = [pick(upper, ours, theirs) for theirs, ours in zip(other, mine)]
    product = times(low[0], high[0])
    forward = plus(times(high[0], low[1]), high[1])
    backward = plus(times_conj(low[0], high[2]), low[2])
    total_out[...] = jnp.concatenate([*product, *forward, *backward, *product], axis=0)


def states_kernel(
    bit,
    decay_ref,
    chunk_ref,
    fwd_re,
    fwd_im,
    fwd_are,
    fwd_aim,
    back_re,
    back_im,
    back_are,
    back_aim,
    outside_ref,
    other_ref,
    in_ref,
    cot_ref,
    state_ref,
    adjoint_ref,
    grad_ref,
):
    rows, states = fwd_re.shape
    groups = rows // GROUP
    dp_place = places()[1]
    gain = gain_of(decay_ref[...])
    outside = widen(bit, pairs_of(outside_ref[...]), pairs_of(other_ref[...]))
    (f_re, f_im), (b_re, b_im) = outside[1], outside[3]
    chunk_of = lambda slot, chunk: chunk_ref[slot, chunk : chunk + 1, :]
    f_starts, b_starts = [], []
    for chunk in range(groups * CHUNKS):
        f_starts.append((f_re, f_im))
        l_re, l_im = chunk_of(0, chunk), chunk_of(1, chunk)
        f_re, f_im = (
            l_re * f_re - l_im * f_im + chunk_of(2, chunk),
            l_re * f_im + l_im * f_re + chunk_of(3, chunk),
        )
    for chunk in reversed(range(groups * CHUNKS)):
        b_starts.insert(0, (b_re, b_im))
        l_re, l_im = chunk_of(0, chunk), chunk_of(1, chunk)
        b_re, b_im = (
            l_re * b_re + l_im * b_im + chunk_of(4, chunk),
            l_re * b_im - l_im * b_re + chunk_of(5, chunk),
        )
    for starts, re_ref, im_ref, are_ref, aim_ref, pairs_ref, scale in (
        (f_starts, fwd_re, fwd_im, fwd_are, fwd_aim, state_ref, None),
        (b_starts, back_re, back_im, back_are, back_aim, adjoint_ref, gain),
    ):
        for group in range(groups):
            mine = starts[group * CHUNKS : (group + 1) * CHUNKS]
            c_re = jnp.concatenate([start[0] for start in mine], axis=0)
            c_im = jnp.concatenate([start[1] for start in mine], axis=0)
            for first in range(group * GROUP, (group + 1) * GROUP, 2 * CHUNKS):
                part = pl.ds(first, 2 * CHUNKS)
                two = lambda value: jnp.concatenate([value, value], axis=0)
                a_re, a_im = are_ref[part, :], aim_ref[part, :]
                s_re = re_ref[part, :] + a_re * two(c_re) - a_im * two(c_im)
                s_im = im_ref[part, :] + a_re * two(c_im) + a_im * two(c_re)
                if scale is not None:
                    s_re, s_im = s_re * scale, s_im * scale
                pairs_ref[part, pl.ds(0, states)] = s_re.astype(jnp.bfloat16)
                pairs_ref[part, pl.ds(states, states)] = s_im.astype(jnp.bfloat16)
    grad_part(dp_place & 1 == 1, in_ref, cot_ref, state_ref, adjoint_ref, 0, grad_ref)


def grad_part(of_input, in_ref, cot_ref, state_ref, adjoint_ref, half, grad_ref):
    columns = pl.ds(half * grad_ref.shape[1], grad_ref.shape[1])
    over_rows = (((0,), (0,)), ((), ()))

    @pl.when(of_input)
    def _():
        grad_ref[...] = lax.dot_general(
            in_ref[...], adjoint_ref[:, columns], over_rows, preferred_element_type=jnp.float32
        )

    @pl.when(jnp.logical_not(of_input))
    def _():
        grad_ref[...] = lax.dot_general(
            cot_ref[...], state_ref[:, columns], over_rows, preferred_element_type=jnp.float32
        )


def grads_kernel(plan, in_ref, cot_ref, state_ref, adjoint_ref, *grad_refs):
    core = places()[1] & 1
    for (own, half), grad_ref in zip(plan, grad_refs):
        grad_part((core == 0) == own, in_ref, cot_ref, state_ref, adjoint_ref, half, grad_ref)


def grads(plan, flat_in, flat_cot, state_pairs, adjoint_pairs):
    rows, width = flat_in.shape
    states = state_pairs.shape[1] // 2
    return call(
        functools.partial(grads_kernel, plan),
        "grads",
        [held((width, states))] * len(plan),
        flat_in,
        flat_cot,
        state_pairs,
        adjoint_pairs,
        flops=2 * rows * width * states * len(plan),
    )


def global_states(bit, decay, chunk_totals, planes, outside, other, flat_in, flat_cot):
    rows, width = flat_in.shape
    states = decay.shape[1]
    return call(
        functools.partial(states_kernel, bit),
        "global_states",
        [
            held((rows, 2 * states), jnp.bfloat16),
            held((rows, 2 * states), jnp.bfloat16),
            held((width, states)),
        ],
        decay,
        chunk_totals,
        *planes,
        outside,
        other,
        flat_in,
        flat_cot,
        flops=2 * rows * width * 2 * states,
    )


def products_kernel(
    in_ref,
    cot_ref,
    state_ref,
    adjoint_ref,
    in_proj_ref,
    out_proj_ref,
    skip_ref,
    after_ref,
    out_hbm,
    back_hbm,
    token_ref,
    out_ref,
    back_ref,
    sems,
):
    over_states = (((1,), (1,)), ((), ()))
    token_ref[...] = jnp.zeros_like(token_ref)
    skip = skip_ref[...]
    to_time = shuffle(back=True)
    stores = []
    for slot, (pairs, proj, skipped, target, result) in enumerate(
        (
            (state_ref, out_proj_ref, in_ref, out_ref, out_hbm),
            (adjoint_ref, in_proj_ref, cot_ref, back_ref, back_hbm),
        )
    ):
        mixed = lax.dot_general(
            pairs[...], proj[...], over_states, preferred_element_type=jnp.float32
        )
        mixed = (mixed + skip * skipped[...].astype(jnp.float32)).astype(jnp.bfloat16)
        for first in range(0, mixed.shape[0], GROUP):
            target[pl.ds(first, GROUP), :] = jnp.dot(
                to_time, mixed[first : first + GROUP], preferred_element_type=jnp.float32
            ).astype(jnp.bfloat16)
        stores.append(pltpu.make_async_copy(target, result, sems.at[slot]))
        stores[-1].start()
    for store in stores:
        store.wait()


def products(
    flat_in, flat_cot, state_pairs, adjoint_pairs, input_proj, output_proj, skip_gain, after
):
    rows, width = flat_in.shape
    vmem = pl.BlockSpec(memory_space=pltpu.VMEM)
    hbm = pl.BlockSpec(memory_space=pltpu.HBM)
    return call(
        products_kernel,
        "products",
        [
            jax.ShapeDtypeStruct(flat_in.shape, jnp.bfloat16),
            jax.ShapeDtypeStruct(flat_in.shape, jnp.bfloat16),
            held((8, LANES)),
        ],
        flat_in,
        flat_cot,
        state_pairs,
        adjoint_pairs,
        input_proj,
        output_proj,
        skip_gain,
        after,
        inputs=[vmem] * 7 + [pl.BlockSpec(memory_space=pl.ANY)],
        outputs=[hbm, hbm, vmem],
        scratch=[
            pltpu.VMEM(flat_in.shape, jnp.bfloat16),
            pltpu.VMEM(flat_in.shape, jnp.bfloat16),
            pltpu.SemaphoreType.DMA((2,)),
        ],
        flops=4 * rows * width * state_pairs.shape[1],
    )


def own_bit(step):
    axis, bit = step
    return (lax.axis_index(axis) >> bit) & 1


def add_kernel(layouts, columns, settled, sent, scale, count, *refs):
    sources, out = refs[:count], refs[-1]
    is_zero = (lax.axis_index("dp") & 1) == 0
    indices = []
    for core in range(2):
        free = [s for s in layouts[-1][core] if s not in settled[core] and s != sent[core]]
        fixed = {step: own_bit(step) for step in settled[core]}
        if sent[core] is not None:
            fixed[sent[core]] = 1 - own_bit(sent[core])
        indices.append([])
        for block in range(2 ** len(free)):
            values = dict(fixed)
            for place, step in enumerate(free):
                values[step] = (block >> (len(free) - 1 - place)) & 1
            indices[core].append([])
            for layout in layouts:
                index = 0
                for step in layout[core]:
                    index = index * 2 + values[step]
                indices[core][-1].append(index)
    for block, both in enumerate(zip(*indices)):
        total = None
        for source, zero, one in zip(sources, *both):
            index = jnp.where(is_zero, zero, one)
            wide = source.shape[2] != columns[1] - columns[0]
            part = source[index, :, columns[0] : columns[1]] if wide else source[index]
            total = part if total is None else total + part
        out[block] = total if scale is None else total * scale


def gather_kernel(items, *refs):
    in_ref, out_ref = refs[-2:]
    dp_place = places()[1]
    for (columns, offset), share in zip(items, refs[:-2]):
        place = dp_place ^ offset
        for core, target in enumerate((in_ref, out_ref)):

            @pl.when(place & 1 == core)
            def _():
                target[place >> 1, :, columns[0] : columns[1]] = share[0]


def on_device(
    inputs, step_size, decay_rate, frequency, input_proj, output_proj, skip_gain, cotangent
):
    batch_count, row_count, model_width = inputs.shape
    state_count = decay_rate.shape[0]
    dp_count, context_count = lax.axis_size("dp"), lax.axis_size("context")
    dp_bits, context_bits = dp_count.bit_length() - 1, context_count.bit_length() - 1

    def swap(array, *steps):
        pairs = []
        for dp in range(dp_count):
            axis, bit = steps[dp & (len(steps) - 1)]
            for context in range(context_count):
                if axis == "dp":
                    partner = (dp ^ (1 << bit)) * context_count + context
                else:
                    partner = dp * context_count + (context ^ (1 << bit))
                pairs.append((dp * context_count + context, partner))
        return lax.ppermute(array, ("dp", "context"), pairs)

    *planes, chunk_totals, total, outside, flat_in, flat_cot, in_proj, out_proj, decay = local_scan(
        step_size,
        decay_rate.reshape(1, state_count),
        frequency.reshape(1, state_count),
        inputs.reshape(row_count, model_width),
        cotangent.reshape(row_count, model_width),
        input_proj,
        output_proj,
    )
    for bit in range(context_bits - 1):
        other = swap(total, ("context", bit))
        total, outside = call(
            functools.partial(combine_kernel, bit),
            "combine",
            [held(total.shape), held(outside.shape)],
            total,
            outside,
            other,
        )
    last = context_bits - 1
    state_pairs, adjoint_pairs, lent = global_states(
        last, decay, chunk_totals, planes, outside, swap(total, ("context", last)), flat_in, flat_cot
    )
    sides = (flat_in, flat_cot, state_pairs, adjoint_pairs)
    borrowed = [swap(lent, ("dp", 0))]
    kept, lent = grads(((True, 0), (False, 1)), *sides)
    borrowed.append(swap(lent, ("dp", 0)))
    kept = [kept, *grads(((True, 1),), *sides)]

    extra_bits = [("dp", bit) for bit in range(1, dp_bits)]
    piece = model_width // (context_count * dp_count // 2)
    layout = [("context", bit) for bit in reversed(range(context_bits))] + extra_bits[::-1]
    blocks = (2 ** len(layout), piece, state_count)
    grad_scale = float(batch_count * row_count * dp_count * context_count) ** (-0.5)
    z_bits = [("context", bit) for bit in range(1, context_bits)]
    y_bits = [("context", 0)]
    by_name = {"x": extra_bits, "y": y_bits, "z": z_bits, "Z": z_bits[::-1]}
    streams = []
    for first, past, *names in STREAMS:
        half = first * LANES // state_count
        columns = (first * LANES - half * state_count, past * LANES - half * state_count)
        streams.append(
            {
                "columns": columns,
                "at": first * LANES,
                "sources": [kept[half].reshape(blocks), borrowed[half].reshape(blocks)],
                "layouts": [(layout, layout)] * 2,
                "settled": ([], []),
                "orders": [[step for name in order for step in by_name[name]] for order in names],
            }
        )

    vmem, anywhere = pl.BlockSpec(memory_space=pltpu.VMEM), pl.BlockSpec(memory_space=pl.ANY)

    def add(stream, sent=(None, None), scale=None, later=()):
        free = len(layout) - len(stream["settled"][0]) - (sent[0] is not None)
        width = stream["columns"][1] - stream["columns"][0]
        return call(
            functools.partial(
                add_kernel,
                stream["layouts"],
                stream["columns"],
                stream["settled"],
                sent,
                scale,
                len(stream["sources"]),
            ),
            "halve" if scale is None else "share",
            held((2**free, piece, width)),
            *stream["sources"],
            *later,
            inputs=[vmem] * len(stream["sources"]) + [anywhere] * len(later),
        )

    token = ()
    for place in range(len(layout)):
        for stream in streams:
            steps = [order[place] for order in stream["orders"]]
            away = add(stream, steps, later=token if place == 1 else ())
            stream["settled"] = tuple(
                settled + [step] for settled, step in zip(stream["settled"], steps)
            )
            stream["sources"] = stream["sources"] + [swap(away, *steps)]
            left = tuple(
                [step for step in layout if step not in settled] for settled in stream["settled"]
            )
            stream["layouts"] = stream["layouts"] + [left]
        if place == 0:
            outputs, input_grad, *token = products(
                flat_in,
                flat_cot,
                state_pairs,
                adjoint_pairs,
                in_proj,
                out_proj,
                skip_gain.reshape(1, model_width),
                away,
            )
    items, shares = [], []
    for stream in streams:
        mine = [(0, add(stream, scale=grad_scale))]
        for bit in [bit for _, bit in extra_bits] + [0]:
            mine = mine + [
                (offset ^ (1 << bit), swap(share, ("dp", bit))) for offset, share in mine
            ]
        width = stream["columns"][1] - stream["columns"][0]
        for offset, share in mine:
            items.append(((stream["at"], stream["at"] + width), offset))
            shares.append(share)
    whole = jax.ShapeDtypeStruct((dp_count // 2, piece, 2 * state_count), jnp.float32)
    sums = call(functools.partial(gather_kernel, items), "gather", [whole, whole], *shares)
    sums = [part.reshape(model_width // context_count, 2 * state_count) for part in sums]
    return (outputs.reshape(inputs.shape), input_grad.reshape(inputs.shape), *sums)


def solution(mesh):
    in_specs = (
        P("dp", "context", None),
        P("dp", "context"),
        P(),
        P(),
        P(),
        P(),
        P(),
        P("dp", "context", None),
    )
    out_specs = (
        P("dp", "context", None),
        P("dp", "context", None),
        P("context", None),
        P("context", None),
    )
    return jax.shard_map(
        on_device, mesh=mesh, in_specs=in_specs, out_specs=out_specs, check_vma=False
    )
```

```python
import functools

import jax
import jax.numpy as jnp
from jax import lax
from jax.experimental import pallas as pl
from jax.experimental.pallas import tpu as pltpu
from jax.sharding import PartitionSpec as P

CHUNKS = 8
LANES = 128
GROUP = 256
LOAD_PIECES = 1
VMEM_LIMIT = 24 * 1024 * 1024
STREAMS = ((3, "xyz", "yzx"), (6, "xyz", "yzx"), (8, "xyz", "yzx"))

TWO_OVER_PI = 0.6366197723675814
PIO2_HIGH = 1.5703125
PIO2_MID = 0.0004837512969970703
PIO2_LOW = 7.549789948768648e-08


def sin_cos(angle):
    quadrant_real = jnp.floor(angle * TWO_OVER_PI + 0.5)
    rest = angle - quadrant_real * PIO2_HIGH
    rest = rest - quadrant_real * PIO2_MID
    rest = rest - quadrant_real * PIO2_LOW
    square = rest * rest
    sine = rest + rest * square * (
        -1.6666654611e-1 + square * (8.3321608736e-3 + square * -1.9515295891e-4)
    )
    cosine = (
        1.0
        - 0.5 * square
        + square
        * square
        * (4.166664568298827e-2 + square * (-1.388731625493765e-3 + square * 2.443315711809948e-5))
    )
    quadrant = quadrant_real.astype(jnp.int32)
    swapped = (quadrant & 1) == 1
    sin_base = jnp.where(swapped, cosine, sine)
    cos_base = jnp.where(swapped, sine, cosine)
    sin_value = jnp.where((quadrant & 2) == 2, -sin_base, sin_base)
    cos_value = jnp.where(((quadrant + 1) & 2) == 2, -cos_base, cos_base)
    return sin_value, cos_value


def gain_of(decay):
    twice = 2.0 * decay
    series = 1.0 / 3628800.0
    for factorial in (362880.0, 40320.0, 5040.0, 720.0, 120.0, 24.0, 6.0, 2.0, 1.0):
        series = 1.0 / factorial - twice * series
    return jnp.sqrt(jnp.where(twice < 0.5, twice * series, 1.0 - jnp.exp(-twice)))


def places():
    return lax.axis_index("context"), lax.axis_index("dp")


def shuffle(back=False):
    length = GROUP // CHUNKS
    scan = lax.broadcasted_iota(jnp.int32, (GROUP, GROUP), 1 if back else 0)
    time = lax.broadcasted_iota(jnp.int32, (GROUP, GROUP), 0 if back else 1)
    return jnp.where(time == (scan % CHUNKS) * length + scan // CHUNKS, 1.0, 0.0).astype(
        jnp.bfloat16
    )


def local_scan_kernel(
    step_hbm,
    decay_hbm,
    frequency_hbm,
    in_hbm,
    cot_hbm,
    in_proj_hbm,
    out_proj_hbm,
    lam_re,
    lam_im,
    drive,
    adjoint,
    chunk_ref,
    summary_ref,
    outside_ref,
    in_vmem,
    cot_vmem,
    in_proj_vmem,
    out_proj_vmem,
    decay_ref,
    step_ref,
    frequency_ref,
    in_time,
    cot_time,
    sems,
):
    rows = in_vmem.shape[0]
    groups = rows // GROUP
    length = GROUP // CHUNKS
    states = decay_ref.shape[1]
    small = [
        pltpu.make_async_copy(source, target, sems.at[slot])
        for slot, (source, target) in enumerate(
            ((step_hbm, step_ref), (decay_hbm, decay_ref), (frequency_hbm, frequency_ref))
        )
    ]
    loads = []
    for array, (source, target) in enumerate(
        (
            (in_hbm, in_time),
            (in_proj_hbm, in_proj_vmem),
            (cot_hbm, cot_time),
            (out_proj_hbm, out_proj_vmem),
        )
    ):
        count = source.shape[0] // LOAD_PIECES
        loads.append(
            [
                pltpu.make_async_copy(
                    source.at[pl.ds(piece * count, count)],
                    target.at[pl.ds(piece * count, count)],
                    sems.at[3 + array * LOAD_PIECES + piece],
                )
                for piece in range(LOAD_PIECES)
            ]
        )
    for copy in small + [copy for load in loads[:2] for copy in load]:
        copy.start()
    for copy in small:
        copy.wait()
    decay = decay_ref[...]
    frequency = frequency_ref[...]
    gain = gain_of(decay)
    steps = [
        jnp.concatenate(
            [
                step_ref[:, first : first + length]
                for first in range(group * GROUP, (group + 1) * GROUP, length)
            ],
            axis=0,
        )
        for group in range(groups)
    ]
    for place in range(length):
        for group in range(groups):
            here = jnp.broadcast_to(steps[group][:, place : place + 1], (CHUNKS, states))
            damping = jnp.exp(-here * decay)
            sine, cosine = sin_cos(here * frequency)
            tile = pl.ds(group * GROUP + place * CHUNKS, CHUNKS)
            lam_re[tile, :] = damping * cosine
            lam_im[tile, :] = damping * sine
    for copy in [copy for load in loads[2:] for copy in load]:
        copy.start()
    to_scan = shuffle()
    pair_gain = jnp.concatenate([gain, gain], axis=1)
    for load, time_ref, scan_ref, proj_ref, target in (
        (loads[:2], in_time, in_vmem, in_proj_vmem, drive),
        (loads[2:], cot_time, cot_vmem, out_proj_vmem, adjoint),
    ):
        for copy in load[0]:
            copy.wait()
        for group in range(groups):
            part = pl.ds(group * GROUP, GROUP)
            scan_ref[part, :] = jnp.dot(
                to_scan, time_ref[part, :], preferred_element_type=jnp.float32
            ).astype(jnp.bfloat16)
        for copy in load[1]:
            copy.wait()
        driven = jnp.dot(scan_ref[...], proj_ref[...], preferred_element_type=jnp.float32)
        target[...] = driven * pair_gain if target is drive else driven
    re_cols, im_cols = pl.ds(0, states), pl.ds(states, states)

    def body(place, carry):
        results = []
        for group in range(groups):
            a_re, a_im, f_re, f_im, b_re, b_im = carry[6 * group : 6 * group + 6]
            first = group * GROUP + place * CHUNKS
            tile = pl.ds(pl.multiple_of(first, CHUNKS), CHUNKS)
            lam = lam_re[tile, :], lam_im[tile, :]
            a_re, a_im = times(lam, (a_re, a_im))
            f_re, f_im = plus(times(lam, (f_re, f_im)), (drive[tile, re_cols], drive[tile, im_cols]))
            added = times_conj((a_re, a_im), (adjoint[tile, re_cols], adjoint[tile, im_cols]))
            results += [a_re, a_im, f_re, f_im, b_re + added[0], b_im + added[1]]
        return tuple(results)

    zero = jnp.zeros((CHUNKS, states), jnp.float32)
    one = jnp.ones((CHUNKS, states), jnp.float32)
    totals = lax.fori_loop(0, length, body, (one, zero, zero, zero, zero, zero) * groups, unroll=4)
    parts = [totals[6 * group : 6 * group + 6] for group in range(groups)]
    for group in range(groups):
        for slot, part in enumerate(parts[group]):
            chunk_ref[slot, pl.ds(group * CHUNKS, CHUNKS), :] = part
    rows_of = [
        [part[chunk : chunk + 1, :] for part in parts[group]]
        for group in range(groups)
        for chunk in range(CHUNKS)
    ]
    t_are, t_aim, t_re, t_im = rows_of[0][:4]
    for l_re, l_im, d_re, d_im, _, _ in rows_of[1:]:
        t_are, t_aim = l_re * t_are - l_im * t_aim, l_re * t_aim + l_im * t_are
        t_re, t_im = l_re * t_re - l_im * t_im + d_re, l_re * t_im + l_im * t_re + d_im
    u_re, u_im = rows_of[-1][4:]
    for l_re, l_im, _, _, d_re, d_im in rows_of[-2::-1]:
        u_re, u_im = l_re * u_re + l_im * u_im + d_re, l_re * u_im - l_im * u_re + d_im
    summary_ref[...] = jnp.concatenate(
        [t_are, t_aim, t_re, t_im, u_re, u_im, t_are, t_aim], axis=0
    )
    one, zero = jnp.ones_like(t_are), jnp.zeros_like(t_are)
    outside_ref[...] = jnp.concatenate([one, zero, zero, zero] * 2, axis=0)


def held(shape, dtype=jnp.float32):
    return pltpu.VMEM(shape, dtype)


def call(kernel, name, out_shape, *args, inputs=None, outputs=None, scratch=(), flops=0):
    vmem = pl.BlockSpec(memory_space=pltpu.VMEM)
    return pl.pallas_call(
        kernel,
        out_shape=out_shape,
        in_specs=inputs or [vmem] * len(args),
        out_specs=outputs or jax.tree.map(lambda _: vmem, out_shape),
        scratch_shapes=scratch,
        compiler_params=pltpu.CompilerParams(vmem_limit_bytes=VMEM_LIMIT),
        cost_estimate=pl.CostEstimate(
            flops=flops, bytes_accessed=max(flops // 1000, 1024), transcendentals=0
        ),
        name=name,
    )(*args)


def local_scan(step_row, decay, frequency, flat_in, flat_cot, input_proj, output_proj):
    rows = flat_in.shape[0]
    states = decay.shape[1]
    args = [
        pltpu.with_memory_space_constraint(array, pltpu.HBM)
        for array in (step_row, decay, frequency, flat_in, flat_cot, input_proj, output_proj)
    ]
    return call(
        local_scan_kernel,
        "local_scan",
        [held((rows, states))] * 2
        + [held((rows, 2 * states))] * 2
        + [held((6, rows // GROUP * CHUNKS, states)), held((8, states)), held((8, states))]
        + [held(array.shape, array.dtype) for array in args[3:]]
        + [held(decay.shape)],
        *args,
        inputs=[pl.BlockSpec(memory_space=pltpu.HBM)] * 7,
        scratch=[
            pltpu.VMEM(step_row.shape, jnp.float32),
            pltpu.VMEM(frequency.shape, jnp.float32),
            pltpu.VMEM(flat_in.shape, flat_in.dtype),
            pltpu.VMEM(flat_cot.shape, flat_cot.dtype),
            pltpu.SemaphoreType.DMA((3 + 4 * LOAD_PIECES,)),
        ],
        flops=4 * rows * flat_in.shape[1] * 2 * states,
    )


def planes_kernel(skipped, lam_re, lam_im, drive, adjoint, *rest):
    fwd_re, fwd_im, fwd_are, fwd_aim, back_re, back_im, back_are, back_aim = rest[skipped:]
    rows, states = lam_re.shape
    groups, length = rows // GROUP, GROUP // CHUNKS
    re_cols, im_cols = pl.ds(0, states), pl.ds(states, states)

    def body(place, carry):
        results = []
        for group in range(groups):
            f_are, f_aim, f_re, f_im, b_are, b_aim, b_re, b_im = carry[8 * group : 8 * group + 8]
            first = group * GROUP + place * CHUNKS
            tile = pl.ds(pl.multiple_of(first, CHUNKS), CHUNKS)
            l_re, l_im = lam_re[tile, :], lam_im[tile, :]
            new_are = l_re * f_are - l_im * f_aim
            new_aim = l_re * f_aim + l_im * f_are
            new_re = l_re * f_re - l_im * f_im + drive[tile, re_cols]
            new_im = l_re * f_im + l_im * f_re + drive[tile, im_cols]
            fwd_are[tile, :] = new_are
            fwd_aim[tile, :] = new_aim
            fwd_re[tile, :] = new_re
            fwd_im[tile, :] = new_im
            first = group * GROUP + (length - 1 - place) * CHUNKS
            tile = pl.ds(pl.multiple_of(first, CHUNKS), CHUNKS)
            l_re, l_im = lam_re[tile, :], lam_im[tile, :]
            a_re = b_re + adjoint[tile, re_cols]
            a_im = b_im + adjoint[tile, im_cols]
            back_are[tile, :] = b_are
            back_aim[tile, :] = b_aim
            back_re[tile, :] = a_re
            back_im[tile, :] = a_im
            results += [
                new_are,
                new_aim,
                new_re,
                new_im,
                l_re * b_are + l_im * b_aim,
                l_re * b_aim - l_im * b_are,
                l_re * a_re + l_im * a_im,
                l_re * a_im - l_im * a_re,
            ]
        return tuple(results)

    zero = jnp.zeros((CHUNKS, states), jnp.float32)
    one = jnp.ones((CHUNKS, states), jnp.float32)
    lax.fori_loop(
        0, length, body, (one, zero, zero, zero, one, zero, zero, zero) * groups, unroll=4
    )


def planes_of(lam_re, lam_im, drive, adjoint, *after):
    vmem = pl.BlockSpec(memory_space=pltpu.VMEM)
    return call(
        functools.partial(planes_kernel, len(after)),
        "planes",
        [held(lam_re.shape)] * 8,
        lam_re,
        lam_im,
        drive,
        adjoint,
        *after,
        inputs=[vmem] * 4 + [pl.BlockSpec(memory_space=pl.ANY)] * len(after),
    )


def times(a, b):
    return a[0] * b[0] - a[1] * b[1], a[0] * b[1] + a[1] * b[0]


def times_conj(a, b):
    return a[0] * b[0] + a[1] * b[1], a[0] * b[1] - a[1] * b[0]


def plus(a, b):
    return a[0] + b[0], a[1] + b[1]


def pick(upper, a, b):
    return tuple(jnp.where(upper, x, y) for x, y in zip(a, b))


def pairs_of(array):
    return [(array[row : row + 1], array[row + 1 : row + 2]) for row in range(0, 8, 2)]


def widen(bit, outside, other):
    upper = ((lax.axis_index("context") >> bit) & 1) == 1
    below, below_sum, above, above_sum = outside
    product, forward, backward, _ = other
    return (
        pick(upper, times(below, product), below),
        pick(upper, plus(times(below, forward), below_sum), below_sum),
        pick(upper, above, times(above, product)),
        pick(upper, above_sum, plus(times_conj(above, backward), above_sum)),
    )


def combine_kernel(bit, total_ref, outside_ref, other_ref, total_out, outside_out):
    other = pairs_of(other_ref[...])
    mine = pairs_of(total_ref[...])
    outside = widen(bit, pairs_of(outside_ref[...]), other)
    outside_out[...] = jnp.concatenate([part for pair in outside for part in pair], axis=0)
    upper = ((lax.axis_index("context") >> bit) & 1) == 1
    low = [pick(upper, theirs, ours) for theirs, ours in zip(other, mine)]
    high = [pick(upper, ours, theirs) for theirs, ours in zip(other, mine)]
    product = times(low[0], high[0])
    forward = plus(times(high[0], low[1]), high[1])
    backward = plus(times_conj(low[0], high[2]), low[2])
    total_out[...] = jnp.concatenate([*product, *forward, *backward, *product], axis=0)


def pairs_into(forward, chunk_ref, outside, gain, re_ref, im_ref, are_ref, aim_ref, pairs_ref):
    rows, states = re_ref.shape
    groups = rows // GROUP
    c_re, c_im = outside[1] if forward else outside[3]
    starts = {}
    chunks = range(groups * CHUNKS)
    for chunk in chunks if forward else reversed(chunks):
        starts[chunk] = (c_re, c_im)
        part = lambda slot: chunk_ref[slot, chunk : chunk + 1, :]
        factor, added = (part(0), part(1)), (part(2), part(3)) if forward else (part(4), part(5))
        c_re, c_im = plus((times if forward else times_conj)(factor, (c_re, c_im)), added)
    for group in range(groups):
        mine = [starts[group * CHUNKS + chunk] for chunk in range(CHUNKS)]
        c_re = jnp.concatenate([start[0] for start in mine] * 2, axis=0)
        c_im = jnp.concatenate([start[1] for start in mine] * 2, axis=0)
        for first in range(group * GROUP, (group + 1) * GROUP, 2 * CHUNKS):
            part = pl.ds(first, 2 * CHUNKS)
            a_re, a_im = are_ref[part, :], aim_ref[part, :]
            s_re = re_ref[part, :] + a_re * c_re - a_im * c_im
            s_im = im_ref[part, :] + a_re * c_im + a_im * c_re
            if not forward:
                s_re, s_im = s_re * gain, s_im * gain
            pairs_ref[part, pl.ds(0, states)] = s_re.astype(jnp.bfloat16)
            pairs_ref[part, pl.ds(states, states)] = s_im.astype(jnp.bfloat16)


def side_kernel(own, bit, parts, skipped, *refs):
    decay_ref, chunk_ref, *planes_refs = refs[:10]
    outside_ref, other_ref, in_ref, cot_ref = refs[10:14]
    pairs_ref, *outs, grad_ref = refs[14 + skipped :]
    core = places()[1] & 1
    of_input = core == (0 if own else 1)
    outside = widen(bit, pairs_of(outside_ref[...]), pairs_of(other_ref[...]))
    over_rows = (((0,), (0,)), ((), ()))
    for forward, rows_ref, planes in (
        (True, cot_ref, planes_refs[:4]),
        (False, in_ref, planes_refs[4:]),
    ):

        @pl.when(of_input != forward)
        def _():
            gain = gain_of(decay_ref[...])
            pairs_into(forward, chunk_ref, outside, gain, *planes, pairs_ref)
            grad_ref[...] = lax.dot_general(
                rows_ref[...], pairs_ref[...], over_rows, preferred_element_type=jnp.float32
            ).reshape(grad_ref.shape)

    for (layout, steps, far, first, past), out in zip(parts, outs):
        for block, both in enumerate(
            zip(*(block_indices(layout, [], step, far) for step in steps[::-1]))
        ):
            out[block] = grad_ref[jnp.where(core == 0, *both), first:past, :]


def side(own, bit, parts, piece, decay, chunk_totals, planes, outside, other, flat_in, flat_cot, after):
    rows, width = flat_in.shape
    states = decay.shape[1]
    args = [decay, chunk_totals, *planes, outside, other, flat_in, flat_cot, *after]
    blocks = (width // piece, piece, 2 * states)
    vmem = pl.BlockSpec(memory_space=pltpu.VMEM)
    shapes = [held((rows, 2 * states), jnp.bfloat16)]
    if own:
        shapes.append(held(blocks))
    for _, _, _, first, past in parts:
        shapes.append(held((blocks[0] // 2, past - first, 2 * states)))
    return call(
        functools.partial(side_kernel, own, bit, parts, len(after)),
        "kept" if own else "lent",
        shapes,
        *args,
        inputs=[vmem] * (len(args) - len(after)) + [pl.BlockSpec(memory_space=pl.ANY)] * len(after),
        scratch=() if own else (pltpu.VMEM(blocks, jnp.float32),),
        flops=2 * rows * width * 2 * states,
    )


def products_kernel(
    in_ref,
    cot_ref,
    lent_ref,
    kept_ref,
    in_proj_ref,
    out_proj_ref,
    skip_ref,
    after_ref,
    out_hbm,
    back_hbm,
    token_ref,
    out_ref,
    back_ref,
    sems,
):
    token_ref[...] = jnp.zeros_like(token_ref)
    over_states = (((1,), (1,)), ((), ()))
    skip = skip_ref[...]
    to_time = shuffle(back=True)
    core = places()[1] & 1
    stores = [
        pltpu.make_async_copy(out_ref, out_hbm, sems.at[0]),
        pltpu.make_async_copy(back_ref, back_hbm, sems.at[1]),
    ]
    for slot, (proj, skipped, target) in enumerate(
        ((out_proj_ref, in_ref, out_ref), (in_proj_ref, cot_ref, back_ref))
    ):
        for which, pairs in enumerate((lent_ref, kept_ref)):

            @pl.when((core == slot) == (which == 0))
            def _():
                mixed = lax.dot_general(
                    pairs[...], proj[...], over_states, preferred_element_type=jnp.float32
                )
                mixed = (mixed + skip * skipped[...].astype(jnp.float32)).astype(jnp.bfloat16)
                for first in range(0, mixed.shape[0], GROUP):
                    target[pl.ds(first, GROUP), :] = jnp.dot(
                        to_time, mixed[first : first + GROUP], preferred_element_type=jnp.float32
                    ).astype(jnp.bfloat16)

        stores[slot].start()
    for store in stores:
        store.wait()


def products(
    flat_in, flat_cot, lent_pairs, kept_pairs, input_proj, output_proj, skip_gain, after
):
    rows, width = flat_in.shape
    vmem = pl.BlockSpec(memory_space=pltpu.VMEM)
    hbm = pl.BlockSpec(memory_space=pltpu.HBM)
    return call(
        products_kernel,
        "products",
        [
            jax.ShapeDtypeStruct(flat_in.shape, jnp.bfloat16),
            jax.ShapeDtypeStruct(flat_in.shape, jnp.bfloat16),
            held((8, LANES)),
        ],
        flat_in,
        flat_cot,
        lent_pairs,
        kept_pairs,
        input_proj,
        output_proj,
        skip_gain,
        after,
        inputs=[vmem] * 7 + [pl.BlockSpec(memory_space=pl.ANY)],
        outputs=[hbm, hbm, vmem],
        scratch=[
            pltpu.VMEM(flat_in.shape, jnp.bfloat16),
            pltpu.VMEM(flat_in.shape, jnp.bfloat16),
            pltpu.SemaphoreType.DMA((2,)),
        ],
        flops=4 * rows * width * lent_pairs.shape[1],
    )


def own_bit(step):
    axis, bit = step
    return (lax.axis_index(axis) >> bit) & 1


def block_indices(layout, settled, sent, far, sources=None):
    values = {step: own_bit(step) for step in settled}
    if sent is not None:
        values[sent] = 1 - own_bit(sent) if far else own_bit(sent)
    free = [step for step in layout if step not in values]
    found = []
    for block in range(2 ** len(free)):
        for place, step in enumerate(free):
            values[step] = (block >> (len(free) - 1 - place)) & 1
        indices = []
        for source in sources or [layout]:
            index = 0
            for step in source:
                index = index * 2 + values[step]
            indices.append(index)
        found.append(indices if sources else indices[0])
    return found


def add_kernel(layout, layouts, rows, settled, sent, scale, count, *refs):
    sources, out = refs[:count], refs[-1]
    is_zero = (lax.axis_index("dp") & 1) == 0
    indices = [
        block_indices(layout, settled[core], sent[core], True, layouts[core]) for core in range(2)
    ]
    for block, both in enumerate(zip(*indices)):
        total = None
        for source, zero, one in zip(sources, *both):
            index = jnp.where(is_zero, zero, one)
            whole = source.shape[1] == rows[1] - rows[0]
            part = source[index] if whole else source[index, rows[0] : rows[1], :]
            total = part if total is None else total + part
        out[block] = total if scale is None else total * scale


def gather_kernel(items, *refs):
    in_ref, out_ref = refs[-2:]
    dp_place = places()[1]
    for (rows, offset), share in zip(items, refs[:-2]):
        place = dp_place ^ offset
        for core, target in enumerate((in_ref, out_ref)):

            @pl.when(place & 1 == core)
            def _():
                target[place >> 1, rows[0] : rows[1], :] = share[0]


def on_device(
    inputs, step_size, decay_rate, frequency, input_proj, output_proj, skip_gain, cotangent
):
    batch_count, row_count, model_width = inputs.shape
    state_count = decay_rate.shape[0]
    dp_count, context_count = lax.axis_size("dp"), lax.axis_size("context")
    dp_bits, context_bits = dp_count.bit_length() - 1, context_count.bit_length() - 1

    def swap(array, *steps):
        pairs = []
        for dp in range(dp_count):
            axis, bit = steps[dp & (len(steps) - 1)]
            for context in range(context_count):
                if axis == "dp":
                    partner = (dp ^ (1 << bit)) * context_count + context
                else:
                    partner = dp * context_count + (context ^ (1 << bit))
                pairs.append((dp * context_count + context, partner))
        return lax.ppermute(array, ("dp", "context"), pairs)

    *driven, chunk_totals, total, outside, flat_in, flat_cot, in_proj, out_proj, decay = local_scan(
        step_size,
        decay_rate.reshape(1, state_count),
        frequency.reshape(1, state_count),
        inputs.reshape(row_count, model_width),
        cotangent.reshape(row_count, model_width),
        input_proj,
        output_proj,
    )
    for bit in range(context_bits - 1):
        other = swap(total, ("context", bit))
        total, outside = call(
            functools.partial(combine_kernel, bit),
            "combine",
            [held(total.shape), held(outside.shape)],
            total,
            outside,
            other,
        )
    planes = planes_of(*driven, outside)
    last = context_bits - 1
    other = swap(total, ("context", last))

    extra_bits = [("dp", bit) for bit in range(1, dp_bits)]
    z_bits = [("context", bit) for bit in range(1, context_bits)]
    by_name = {"x": extra_bits, "y": [("context", 0)], "z": z_bits}
    layout = [("context", bit) for bit in reversed(range(context_bits))] + extra_bits[::-1]
    piece = model_width // 2 ** len(layout)
    grad_scale = float(batch_count * row_count * dp_count * context_count) ** (-0.5)
    less = lambda taken: [step for step in layout if step not in taken]
    streams, first, parts = [], 0, []
    for eighths, *names in STREAMS:
        past = max(8, piece * eighths // 64 * 8)
        if past > first:
            orders = [[step for name in order for step in by_name[name]] for order in names]
            streams.append({"rows": (first, past), "orders": orders, "settled": ([], [])})
            steps = [order[0] for order in orders]
            parts += [(layout, steps, far, first, past) for far in (True, False)]
            first = past

    common = (decay, chunk_totals, planes, outside, other, flat_in, flat_cot)
    lent_pairs, *lent = side(False, last, parts, piece, *common, ())
    borrowed = [swap(part, ("dp", 0)) for part in lent]
    kept_pairs, kept = side(True, last, [], piece, *common, lent[:1])

    vmem, anywhere = pl.BlockSpec(memory_space=pltpu.VMEM), pl.BlockSpec(memory_space=pl.ANY)

    def add(stream, sources, sent=(None, None), scale=None, later=()):
        layouts = [[left[core] for _, left in sources] for core in range(2)]
        free = len(layout) - len(stream["settled"][0]) - (sent[0] is not None)
        first, past = stream["rows"]
        return call(
            functools.partial(
                add_kernel,
                layout,
                layouts,
                stream["rows"],
                stream["settled"],
                sent,
                scale,
                len(sources),
            ),
            "halve" if scale is None else "share",
            held((2**free, past - first, 2 * state_count)),
            *(source for source, _ in sources),
            *later,
            inputs=[vmem] * len(sources) + [anywhere] * len(later),
        )

    before = []
    for place in range(len(layout)):
        for number, stream in enumerate(streams):
            steps = [order[place] for order in stream["orders"]]
            if place == 0:
                left = tuple(less([step]) for step in steps)
                far, near = borrowed[2 * number : 2 * number + 2]
                stream["sources"] = [(kept, (layout, layout)), (near, left)]
                away = add(stream, [stream["sources"][0], (far, left)], steps, later=before)
            else:
                away = add(stream, stream["sources"], steps, later=before)
            stream["settled"] = tuple(
                settled + [step] for settled, step in zip(stream["settled"], steps)
            )
            left = tuple(less(settled) for settled in stream["settled"])
            stream["sources"] = stream["sources"] + [(swap(away, *steps), left)]
        if place == 0:
            outputs, input_grad, token = products(
                flat_in,
                flat_cot,
                lent_pairs,
                kept_pairs,
                in_proj,
                out_proj,
                skip_gain.reshape(1, model_width),
                away,
            )
            before = [token]
    items, shares = [], []
    for stream in streams:
        mine = [(0, add(stream, stream["sources"], scale=grad_scale, later=before))]
        before = ()
        for bit in [bit for _, bit in extra_bits] + [0]:
            mine = mine + [
                (offset ^ (1 << bit), swap(share, ("dp", bit))) for offset, share in mine
            ]
        for offset, share in mine:
            items.append((stream["rows"], offset))
            shares.append(share)
    whole = jax.ShapeDtypeStruct((dp_count // 2, piece, 2 * state_count), jnp.float32)
    sums = call(functools.partial(gather_kernel, items), "gather", [whole, whole], *shares)
    sums = [part.reshape(model_width // context_count, 2 * state_count) for part in sums]
    return (outputs.reshape(inputs.shape), input_grad.reshape(inputs.shape), *sums)


def solution(mesh):
    in_specs = (
        P("dp", "context", None),
        P("dp", "context"),
        P(),
        P(),
        P(),
        P(),
        P(),
        P("dp", "context", None),
    )
    out_specs = (
        P("dp", "context", None),
        P("dp", "context", None),
        P("context", None),
        P("context", None),
    )
    return jax.shard_map(
        on_device, mesh=mesh, in_specs=in_specs, out_specs=out_specs, check_vma=False
    )
```

```python
import functools

import jax
import jax.numpy as jnp
from jax import lax
from jax.experimental import pallas as pl
from jax.experimental.pallas import tpu as pltpu
from jax.sharding import PartitionSpec as P

CHUNKS = 8
LANES = 128
GROUP = 256
LOAD_PIECES = 1
VMEM_LIMIT = 24 * 1024 * 1024
STREAMS = ((5, "xyz", "yzx"), (8, "aybX", "yabX"))

TWO_OVER_PI = 0.6366197723675814
PIO2_HIGH = 1.5703125
PIO2_MID = 0.0004837512969970703
PIO2_LOW = 7.549789948768648e-08


def sin_cos(angle):
    quadrant_real = jnp.floor(angle * TWO_OVER_PI + 0.5)
    rest = angle - quadrant_real * PIO2_HIGH
    rest = rest - quadrant_real * PIO2_MID
    rest = rest - quadrant_real * PIO2_LOW
    square = rest * rest
    sine = rest + rest * square * (
        -1.6666654611e-1 + square * (8.3321608736e-3 + square * -1.9515295891e-4)
    )
    cosine = (
        1.0
        - 0.5 * square
        + square
        * square
        * (4.166664568298827e-2 + square * (-1.388731625493765e-3 + square * 2.443315711809948e-5))
    )
    quadrant = quadrant_real.astype(jnp.int32)
    swapped = (quadrant & 1) == 1
    sin_base = jnp.where(swapped, cosine, sine)
    cos_base = jnp.where(swapped, sine, cosine)
    sin_value = jnp.where((quadrant & 2) == 2, -sin_base, sin_base)
    cos_value = jnp.where(((quadrant + 1) & 2) == 2, -cos_base, cos_base)
    return sin_value, cos_value


def gain_of(decay):
    twice = 2.0 * decay
    series = 1.0 / 3628800.0
    for factorial in (362880.0, 40320.0, 5040.0, 720.0, 120.0, 24.0, 6.0, 2.0, 1.0):
        series = 1.0 / factorial - twice * series
    return jnp.sqrt(jnp.where(twice < 0.5, twice * series, 1.0 - jnp.exp(-twice)))


def places():
    return lax.axis_index("context"), lax.axis_index("dp")


def shuffle(back=False):
    length = GROUP // CHUNKS
    scan = lax.broadcasted_iota(jnp.int32, (GROUP, GROUP), 1 if back else 0)
    time = lax.broadcasted_iota(jnp.int32, (GROUP, GROUP), 0 if back else 1)
    return jnp.where(time == (scan % CHUNKS) * length + scan // CHUNKS, 1.0, 0.0).astype(
        jnp.bfloat16
    )


def local_scan_kernel(
    step_hbm,
    decay_hbm,
    frequency_hbm,
    in_hbm,
    cot_hbm,
    in_proj_hbm,
    out_proj_hbm,
    lam_re,
    lam_im,
    drive,
    adjoint,
    chunk_ref,
    summary_ref,
    outside_ref,
    in_vmem,
    cot_vmem,
    in_proj_vmem,
    out_proj_vmem,
    decay_ref,
    step_ref,
    frequency_ref,
    in_time,
    cot_time,
    sems,
):
    rows = in_vmem.shape[0]
    groups = rows // GROUP
    length = GROUP // CHUNKS
    states = decay_ref.shape[1]
    small = [
        pltpu.make_async_copy(source, target, sems.at[slot])
        for slot, (source, target) in enumerate(
            ((step_hbm, step_ref), (decay_hbm, decay_ref), (frequency_hbm, frequency_ref))
        )
    ]
    loads = []
    for array, (source, target) in enumerate(
        (
            (in_hbm, in_time),
            (in_proj_hbm, in_proj_vmem),
            (cot_hbm, cot_time),
            (out_proj_hbm, out_proj_vmem),
        )
    ):
        count = source.shape[0] // LOAD_PIECES
        loads.append(
            [
                pltpu.make_async_copy(
                    source.at[pl.ds(piece * count, count)],
                    target.at[pl.ds(piece * count, count)],
                    sems.at[3 + array * LOAD_PIECES + piece],
                )
                for piece in range(LOAD_PIECES)
            ]
        )
    for copy in small + [copy for load in loads[:2] for copy in load]:
        copy.start()
    for copy in small:
        copy.wait()
    decay = decay_ref[...]
    frequency = frequency_ref[...]
    gain = gain_of(decay)
    steps = [
        jnp.concatenate(
            [
                step_ref[:, first : first + length]
                for first in range(group * GROUP, (group + 1) * GROUP, length)
            ],
            axis=0,
        )
        for group in range(groups)
    ]
    for place in range(length):
        for group in range(groups):
            here = jnp.broadcast_to(steps[group][:, place : place + 1], (CHUNKS, states))
            damping = jnp.exp(-here * decay)
            sine, cosine = sin_cos(here * frequency)
            tile = pl.ds(group * GROUP + place * CHUNKS, CHUNKS)
            lam_re[tile, :] = damping * cosine
            lam_im[tile, :] = damping * sine
    for copy in [copy for load in loads[2:] for copy in load]:
        copy.start()
    to_scan = shuffle()
    pair_gain = jnp.concatenate([gain, gain], axis=1)
    for load, time_ref, scan_ref, proj_ref, target in (
        (loads[:2], in_time, in_vmem, in_proj_vmem, drive),
        (loads[2:], cot_time, cot_vmem, out_proj_vmem, adjoint),
    ):
        for copy in load[0]:
            copy.wait()
        for group in range(groups):
            part = pl.ds(group * GROUP, GROUP)
            scan_ref[part, :] = jnp.dot(
                to_scan, time_ref[part, :], preferred_element_type=jnp.float32
            ).astype(jnp.bfloat16)
        for copy in load[1]:
            copy.wait()
        driven = jnp.dot(scan_ref[...], proj_ref[...], preferred_element_type=jnp.float32)
        target[...] = driven * pair_gain if target is drive else driven
    re_cols, im_cols = pl.ds(0, states), pl.ds(states, states)

    def body(place, carry):
        results = []
        for group in range(groups):
            a_re, a_im, f_re, f_im, b_re, b_im = carry[6 * group : 6 * group + 6]
            first = group * GROUP + place * CHUNKS
            tile = pl.ds(pl.multiple_of(first, CHUNKS), CHUNKS)
            lam = lam_re[tile, :], lam_im[tile, :]
            a_re, a_im = times(lam, (a_re, a_im))
            f_re, f_im = plus(times(lam, (f_re, f_im)), (drive[tile, re_cols], drive[tile, im_cols]))
            added = times_conj((a_re, a_im), (adjoint[tile, re_cols], adjoint[tile, im_cols]))
            results += [a_re, a_im, f_re, f_im, b_re + added[0], b_im + added[1]]
        return tuple(results)

    zero = jnp.zeros((CHUNKS, states), jnp.float32)
    one = jnp.ones((CHUNKS, states), jnp.float32)
    totals = lax.fori_loop(0, length, body, (one, zero, zero, zero, zero, zero) * groups, unroll=4)
    parts = [totals[6 * group : 6 * group + 6] for group in range(groups)]
    for group in range(groups):
        for slot, part in enumerate(parts[group]):
            chunk_ref[slot, pl.ds(group * CHUNKS, CHUNKS), :] = part
    rows_of = [
        [part[chunk : chunk + 1, :] for part in parts[group]]
        for group in range(groups)
        for chunk in range(CHUNKS)
    ]
    t_are, t_aim, t_re, t_im = rows_of[0][:4]
    for l_re, l_im, d_re, d_im, _, _ in rows_of[1:]:
        t_are, t_aim = l_re * t_are - l_im * t_aim, l_re * t_aim + l_im * t_are
        t_re, t_im = l_re * t_re - l_im * t_im + d_re, l_re * t_im + l_im * t_re + d_im
    u_re, u_im = rows_of[-1][4:]
    for l_re, l_im, _, _, d_re, d_im in rows_of[-2::-1]:
        u_re, u_im = l_re * u_re + l_im * u_im + d_re, l_re * u_im - l_im * u_re + d_im
    summary_ref[...] = jnp.concatenate(
        [t_are, t_aim, t_re, t_im, u_re, u_im, t_are, t_aim], axis=0
    )
    one, zero = jnp.ones_like(t_are), jnp.zeros_like(t_are)
    outside_ref[...] = jnp.concatenate([one, zero, zero, zero] * 2, axis=0)


def held(shape, dtype=jnp.float32):
    return pltpu.VMEM(shape, dtype)


def call(kernel, name, out_shape, *args, inputs=None, outputs=None, scratch=(), flops=0):
    vmem = pl.BlockSpec(memory_space=pltpu.VMEM)
    return pl.pallas_call(
        kernel,
        out_shape=out_shape,
        in_specs=inputs or [vmem] * len(args),
        out_specs=outputs or jax.tree.map(lambda _: vmem, out_shape),
        scratch_shapes=scratch,
        compiler_params=pltpu.CompilerParams(vmem_limit_bytes=VMEM_LIMIT),
        cost_estimate=pl.CostEstimate(
            flops=flops, bytes_accessed=max(flops // 1000, 1024), transcendentals=0
        ),
        name=name,
    )(*args)


def local_scan(step_row, decay, frequency, flat_in, flat_cot, input_proj, output_proj):
    rows = flat_in.shape[0]
    states = decay.shape[1]
    args = [
        pltpu.with_memory_space_constraint(array, pltpu.HBM)
        for array in (step_row, decay, frequency, flat_in, flat_cot, input_proj, output_proj)
    ]
    return call(
        local_scan_kernel,
        "local_scan",
        [held((rows, states))] * 2
        + [held((rows, 2 * states))] * 2
        + [held((6, rows // GROUP * CHUNKS, states)), held((8, states)), held((8, states))]
        + [held(array.shape, array.dtype) for array in args[3:]]
        + [held(decay.shape)],
        *args,
        inputs=[pl.BlockSpec(memory_space=pltpu.HBM)] * 7,
        scratch=[
            pltpu.VMEM(step_row.shape, jnp.float32),
            pltpu.VMEM(frequency.shape, jnp.float32),
            pltpu.VMEM(flat_in.shape, flat_in.dtype),
            pltpu.VMEM(flat_cot.shape, flat_cot.dtype),
            pltpu.SemaphoreType.DMA((3 + 4 * LOAD_PIECES,)),
        ],
        flops=4 * rows * flat_in.shape[1] * 2 * states,
    )


def planes_kernel(skipped, lam_re, lam_im, drive, adjoint, *rest):
    fwd_re, fwd_im, fwd_are, fwd_aim, back_re, back_im, back_are, back_aim = rest[skipped:]
    rows, states = lam_re.shape
    groups, length = rows // GROUP, GROUP // CHUNKS
    re_cols, im_cols = pl.ds(0, states), pl.ds(states, states)

    def body(place, carry):
        results = []
        for group in range(groups):
            f_are, f_aim, f_re, f_im, b_are, b_aim, b_re, b_im = carry[8 * group : 8 * group + 8]
            first = group * GROUP + place * CHUNKS
            tile = pl.ds(pl.multiple_of(first, CHUNKS), CHUNKS)
            l_re, l_im = lam_re[tile, :], lam_im[tile, :]
            new_are = l_re * f_are - l_im * f_aim
            new_aim = l_re * f_aim + l_im * f_are
            new_re = l_re * f_re - l_im * f_im + drive[tile, re_cols]
            new_im = l_re * f_im + l_im * f_re + drive[tile, im_cols]
            fwd_are[tile, :] = new_are
            fwd_aim[tile, :] = new_aim
            fwd_re[tile, :] = new_re
            fwd_im[tile, :] = new_im
            first = group * GROUP + (length - 1 - place) * CHUNKS
            tile = pl.ds(pl.multiple_of(first, CHUNKS), CHUNKS)
            l_re, l_im = lam_re[tile, :], lam_im[tile, :]
            a_re = b_re + adjoint[tile, re_cols]
            a_im = b_im + adjoint[tile, im_cols]
            back_are[tile, :] = b_are
            back_aim[tile, :] = b_aim
            back_re[tile, :] = a_re
            back_im[tile, :] = a_im
            results += [
                new_are,
                new_aim,
                new_re,
                new_im,
                l_re * b_are + l_im * b_aim,
                l_re * b_aim - l_im * b_are,
                l_re * a_re + l_im * a_im,
                l_re * a_im - l_im * a_re,
            ]
        return tuple(results)

    zero = jnp.zeros((CHUNKS, states), jnp.float32)
    one = jnp.ones((CHUNKS, states), jnp.float32)
    lax.fori_loop(
        0, length, body, (one, zero, zero, zero, one, zero, zero, zero) * groups, unroll=4
    )


def planes_of(lam_re, lam_im, drive, adjoint, *after):
    vmem = pl.BlockSpec(memory_space=pltpu.VMEM)
    return call(
        functools.partial(planes_kernel, len(after)),
        "planes",
        [held(lam_re.shape)] * 8,
        lam_re,
        lam_im,
        drive,
        adjoint,
        *after,
        inputs=[vmem] * 4 + [pl.BlockSpec(memory_space=pl.ANY)] * len(after),
    )


def times(a, b):
    return a[0] * b[0] - a[1] * b[1], a[0] * b[1] + a[1] * b[0]


def times_conj(a, b):
    return a[0] * b[0] + a[1] * b[1], a[0] * b[1] - a[1] * b[0]


def plus(a, b):
    return a[0] + b[0], a[1] + b[1]


def pick(upper, a, b):
    return tuple(jnp.where(upper, x, y) for x, y in zip(a, b))


def pairs_of(array):
    return [(array[row : row + 1], array[row + 1 : row + 2]) for row in range(0, 8, 2)]


def widen(bit, outside, other):
    upper = ((lax.axis_index("context") >> bit) & 1) == 1
    below, below_sum, above, above_sum = outside
    product, forward, backward, _ = other
    return (
        pick(upper, times(below, product), below),
        pick(upper, plus(times(below, forward), below_sum), below_sum),
        pick(upper, above, times(above, product)),
        pick(upper, above_sum, plus(times_conj(above, backward), above_sum)),
    )


def combine_kernel(bit, total_ref, outside_ref, other_ref, total_out, outside_out):
    other = pairs_of(other_ref[...])
    mine = pairs_of(total_ref[...])
    outside = widen(bit, pairs_of(outside_ref[...]), other)
    outside_out[...] = jnp.concatenate([part for pair in outside for part in pair], axis=0)
    upper = ((lax.axis_index("context") >> bit) & 1) == 1
    low = [pick(upper, theirs, ours) for theirs, ours in zip(other, mine)]
    high = [pick(upper, ours, theirs) for theirs, ours in zip(other, mine)]
    product = times(low[0], high[0])
    forward = plus(times(high[0], low[1]), high[1])
    backward = plus(times_conj(low[0], high[2]), low[2])
    total_out[...] = jnp.concatenate([*product, *forward, *backward, *product], axis=0)


def pairs_into(forward, chunk_ref, outside, gain, re_ref, im_ref, are_ref, aim_ref, pairs_ref):
    rows, states = re_ref.shape
    groups = rows // GROUP
    c_re, c_im = outside[1] if forward else outside[3]
    starts = {}
    chunks = range(groups * CHUNKS)
    for chunk in chunks if forward else reversed(chunks):
        starts[chunk] = (c_re, c_im)
        part = lambda slot: chunk_ref[slot, chunk : chunk + 1, :]
        factor, added = (part(0), part(1)), (part(2), part(3)) if forward else (part(4), part(5))
        c_re, c_im = plus((times if forward else times_conj)(factor, (c_re, c_im)), added)
    for group in range(groups):
        mine = [starts[group * CHUNKS + chunk] for chunk in range(CHUNKS)]
        c_re = jnp.concatenate([start[0] for start in mine] * 2, axis=0)
        c_im = jnp.concatenate([start[1] for start in mine] * 2, axis=0)
        for first in range(group * GROUP, (group + 1) * GROUP, 2 * CHUNKS):
            part = pl.ds(first, 2 * CHUNKS)
            a_re, a_im = are_ref[part, :], aim_ref[part, :]
            s_re = re_ref[part, :] + a_re * c_re - a_im * c_im
            s_im = im_ref[part, :] + a_re * c_im + a_im * c_re
            if not forward:
                s_re, s_im = s_re * gain, s_im * gain
            pairs_ref[part, pl.ds(0, states)] = s_re.astype(jnp.bfloat16)
            pairs_ref[part, pl.ds(states, states)] = s_im.astype(jnp.bfloat16)


def side_kernel(own, bit, parts, skipped, *refs):
    decay_ref, chunk_ref, *planes_refs = refs[:10]
    outside_ref, other_ref, in_ref, cot_ref = refs[10:14]
    pairs_ref, *outs, grad_ref = refs[14 + skipped :]
    core = places()[1] & 1
    of_input = core == (0 if own else 1)
    outside = widen(bit, pairs_of(outside_ref[...]), pairs_of(other_ref[...]))
    over_rows = (((0,), (0,)), ((), ()))
    for forward, rows_ref, planes in (
        (True, cot_ref, planes_refs[:4]),
        (False, in_ref, planes_refs[4:]),
    ):

        @pl.when(of_input != forward)
        def _():
            gain = gain_of(decay_ref[...])
            pairs_into(forward, chunk_ref, outside, gain, *planes, pairs_ref)
            grad_ref[...] = lax.dot_general(
                rows_ref[...], pairs_ref[...], over_rows, preferred_element_type=jnp.float32
            ).reshape(grad_ref.shape)

    for (layout, steps, far, first, past), out in zip(parts, outs):
        for block, both in enumerate(
            zip(*(block_indices(layout, [], step, far) for step in steps[::-1]))
        ):
            out[block] = grad_ref[jnp.where(core == 0, *both), first:past, :]


def side(own, bit, parts, piece, decay, chunk_totals, planes, outside, other, flat_in, flat_cot, after):
    rows, width = flat_in.shape
    states = decay.shape[1]
    args = [decay, chunk_totals, *planes, outside, other, flat_in, flat_cot, *after]
    blocks = (width // piece, piece, 2 * states)
    vmem = pl.BlockSpec(memory_space=pltpu.VMEM)
    shapes = [held((rows, 2 * states), jnp.bfloat16)]
    if own:
        shapes.append(held(blocks))
    for _, _, _, first, past in parts:
        shapes.append(held((blocks[0] // 2, past - first, 2 * states)))
    return call(
        functools.partial(side_kernel, own, bit, parts, len(after)),
        "kept" if own else "lent",
        shapes,
        *args,
        inputs=[vmem] * (len(args) - len(after)) + [pl.BlockSpec(memory_space=pl.ANY)] * len(after),
        scratch=() if own else (pltpu.VMEM(blocks, jnp.float32),),
        flops=2 * rows * width * 2 * states,
    )


def products_kernel(
    in_ref,
    cot_ref,
    lent_ref,
    kept_ref,
    in_proj_ref,
    out_proj_ref,
    skip_ref,
    after_ref,
    out_hbm,
    back_hbm,
    token_ref,
    out_ref,
    back_ref,
    sems,
):
    token_ref[...] = jnp.zeros_like(token_ref)
    over_states = (((1,), (1,)), ((), ()))
    skip = skip_ref[...]
    to_time = shuffle(back=True)
    core = places()[1] & 1
    stores = [
        pltpu.make_async_copy(out_ref, out_hbm, sems.at[0]),
        pltpu.make_async_copy(back_ref, back_hbm, sems.at[1]),
    ]
    for slot, (proj, skipped, target) in enumerate(
        ((out_proj_ref, in_ref, out_ref), (in_proj_ref, cot_ref, back_ref))
    ):
        for which, pairs in enumerate((lent_ref, kept_ref)):

            @pl.when((core == slot) == (which == 0))
            def _():
                mixed = lax.dot_general(
                    pairs[...], proj[...], over_states, preferred_element_type=jnp.float32
                )
                mixed = (mixed + skip * skipped[...].astype(jnp.float32)).astype(jnp.bfloat16)
                for first in range(0, mixed.shape[0], GROUP):
                    target[pl.ds(first, GROUP), :] = jnp.dot(
                        to_time, mixed[first : first + GROUP], preferred_element_type=jnp.float32
                    ).astype(jnp.bfloat16)

        stores[slot].start()
    for store in stores:
        store.wait()


def products(
    flat_in, flat_cot, lent_pairs, kept_pairs, input_proj, output_proj, skip_gain, after
):
    rows, width = flat_in.shape
    vmem = pl.BlockSpec(memory_space=pltpu.VMEM)
    hbm = pl.BlockSpec(memory_space=pltpu.HBM)
    return call(
        products_kernel,
        "products",
        [
            jax.ShapeDtypeStruct(flat_in.shape, jnp.bfloat16),
            jax.ShapeDtypeStruct(flat_in.shape, jnp.bfloat16),
            held((8, LANES)),
        ],
        flat_in,
        flat_cot,
        lent_pairs,
        kept_pairs,
        input_proj,
        output_proj,
        skip_gain,
        after,
        inputs=[vmem] * 7 + [pl.BlockSpec(memory_space=pl.ANY)],
        outputs=[hbm, hbm, vmem],
        scratch=[
            pltpu.VMEM(flat_in.shape, jnp.bfloat16),
            pltpu.VMEM(flat_in.shape, jnp.bfloat16),
            pltpu.SemaphoreType.DMA((2,)),
        ],
        flops=4 * rows * width * lent_pairs.shape[1],
    )


def own_bit(step):
    axis, bit = step
    return (lax.axis_index(axis) >> bit) & 1


def block_indices(layout, settled, sent, far, sources=None):
    values = {step: own_bit(step) for step in settled}
    if sent is not None:
        values[sent] = 1 - own_bit(sent) if far else own_bit(sent)
    free = [step for step in layout if step not in values]
    found = []
    for block in range(2 ** len(free)):
        for place, step in enumerate(free):
            values[step] = (block >> (len(free) - 1 - place)) & 1
        indices = []
        for source in sources or [layout]:
            index = 0
            for step in source:
                index = index * 2 + values[step]
            indices.append(index)
        found.append(indices if sources else indices[0])
    return found


def add_kernel(layout, layouts, rows, settled, sent, scale, count, *refs):
    sources, out = refs[:count], refs[-1]
    is_zero = (lax.axis_index("dp") & 1) == 0
    indices = [
        block_indices(layout, settled[core], sent[core], True, layouts[core]) for core in range(2)
    ]
    for block, both in enumerate(zip(*indices)):
        total = None
        for source, zero, one in zip(sources, *both):
            index = jnp.where(is_zero, zero, one)
            whole = source.shape[1] == rows[1] - rows[0]
            part = source[index] if whole else source[index, rows[0] : rows[1], :]
            total = part if total is None else total + part
        out[block] = total if scale is None else total * scale


def gather_kernel(items, *refs):
    in_ref, out_ref = refs[-2:]
    dp_place = places()[1]
    for (rows, offset), share in zip(items, refs[:-2]):
        place = dp_place ^ offset
        for core, target in enumerate((in_ref, out_ref)):

            @pl.when(place & 1 == core)
            def _():
                if share.shape[0] == target.shape[0]:
                    target[:, rows[0] : rows[1], :] = share[...]
                else:
                    target[place >> 1, rows[0] : rows[1], :] = share[0]


def on_device(
    inputs, step_size, decay_rate, frequency, input_proj, output_proj, skip_gain, cotangent
):
    batch_count, row_count, model_width = inputs.shape
    state_count = decay_rate.shape[0]
    dp_count, context_count = lax.axis_size("dp"), lax.axis_size("context")
    dp_bits, context_bits = dp_count.bit_length() - 1, context_count.bit_length() - 1

    def swap(array, *steps):
        pairs = []
        for dp in range(dp_count):
            axis, bit = steps[dp & (len(steps) - 1)]
            for context in range(context_count):
                if axis == "dp":
                    partner = (dp ^ (1 << bit)) * context_count + context
                else:
                    partner = dp * context_count + (context ^ (1 << bit))
                pairs.append((dp * context_count + context, partner))
        return lax.ppermute(array, ("dp", "context"), pairs)

    *driven, chunk_totals, total, outside, flat_in, flat_cot, in_proj, out_proj, decay = local_scan(
        step_size,
        decay_rate.reshape(1, state_count),
        frequency.reshape(1, state_count),
        inputs.reshape(row_count, model_width),
        cotangent.reshape(row_count, model_width),
        input_proj,
        output_proj,
    )
    for bit in range(context_bits - 1):
        other = swap(total, ("context", bit))
        total, outside = call(
            functools.partial(combine_kernel, bit),
            "combine",
            [held(total.shape), held(outside.shape)],
            total,
            outside,
            other,
        )
    planes = planes_of(*driven, outside)
    last = context_bits - 1
    other = swap(total, ("context", last))

    extra_bits = [("dp", bit) for bit in range(1, dp_bits)]
    z_bits = [("context", bit) for bit in range(1, context_bits)]
    by_name = {
        "x": extra_bits,
        "y": [("context", 0)],
        "z": z_bits,
        "a": z_bits[:1],
        "b": z_bits[1:],
    }
    layout = [("context", bit) for bit in reversed(range(context_bits))] + extra_bits[::-1]
    piece = model_width // 2 ** len(layout)
    grad_scale = float(batch_count * row_count * dp_count * context_count) ** (-0.5)
    less = lambda taken: [step for step in layout if step not in taken]
    streams, first, parts = [], 0, []
    for eighths, *names in STREAMS:
        past = max(8, piece * eighths // 64 * 8)
        if past > first:
            orders = [[step for name in order for step in by_name[name.lower()]] for order in names]
            halvings = len(layout) - (len(extra_bits) if "X" in names[0] else 0)
            streams.append(
                {"rows": (first, past), "orders": orders, "settled": ([], []), "halvings": halvings}
            )
            steps = [order[0] for order in orders]
            parts += [(layout, steps, far, first, past) for far in (True, False)]
            first = past

    common = (decay, chunk_totals, planes, outside, other, flat_in, flat_cot)
    lent_pairs, *lent = side(False, last, parts, piece, *common, ())
    borrowed = [swap(part, ("dp", 0)) for part in lent]
    kept_pairs, kept = side(True, last, [], piece, *common, lent[:1])

    vmem, anywhere = pl.BlockSpec(memory_space=pltpu.VMEM), pl.BlockSpec(memory_space=pl.ANY)

    def add(stream, sources, sent=(None, None), scale=None, later=()):
        layouts = [[left[core] for _, left in sources] for core in range(2)]
        free = len(layout) - len(stream["settled"][0]) - (sent[0] is not None)
        first, past = stream["rows"]
        return call(
            functools.partial(
                add_kernel,
                layout,
                layouts,
                stream["rows"],
                stream["settled"],
                sent,
                scale,
                len(sources),
            ),
            "halve" if scale is None else "share",
            held((2**free, past - first, 2 * state_count)),
            *(source for source, _ in sources),
            *later,
            inputs=[vmem] * len(sources) + [anywhere] * len(later),
        )

    before = []
    for place in range(len(layout)):
        for number, stream in enumerate(streams):
            steps = [order[place] for order in stream["orders"]]
            if place >= stream["halvings"]:
                left = tuple(less(settled) for settled in stream["settled"])
                away = add(stream, stream["sources"], later=before)
                stream["sources"] = [(away, left), (swap(away, *steps), left)]
                continue
            if place == 0:
                left = tuple(less([step]) for step in steps)
                far, near = borrowed[2 * number : 2 * number + 2]
                stream["sources"] = [(kept, (layout, layout)), (near, left)]
                away = add(stream, [stream["sources"][0], (far, left)], steps, later=before)
            else:
                away = add(stream, stream["sources"], steps, later=before)
            stream["settled"] = tuple(
                settled + [step] for settled, step in zip(stream["settled"], steps)
            )
            left = tuple(less(settled) for settled in stream["settled"])
            stream["sources"] = stream["sources"] + [(swap(away, *steps), left)]
        if place == 0:
            outputs, input_grad, token = products(
                flat_in,
                flat_cot,
                lent_pairs,
                kept_pairs,
                in_proj,
                out_proj,
                skip_gain.reshape(1, model_width),
                away,
            )
            before = [token]
    items, shares = [], []
    for stream in streams:
        mine = [(0, add(stream, stream["sources"], scale=grad_scale, later=before))]
        before = ()
        for bit in [bit for _, bit in extra_bits if stream["halvings"] == len(layout)] + [0]:
            mine = mine + [
                (offset ^ (1 << bit), swap(share, ("dp", bit))) for offset, share in mine
            ]
        for offset, share in mine:
            items.append((stream["rows"], offset))
            shares.append(share)
    whole = jax.ShapeDtypeStruct((dp_count // 2, piece, 2 * state_count), jnp.float32)
    sums = call(functools.partial(gather_kernel, items), "gather", [whole, whole], *shares)
    sums = [part.reshape(model_width // context_count, 2 * state_count) for part in sums]
    return (outputs.reshape(inputs.shape), input_grad.reshape(inputs.shape), *sums)


def solution(mesh):
    in_specs = (
        P("dp", "context", None),
        P("dp", "context"),
        P(),
        P(),
        P(),
        P(),
        P(),
        P("dp", "context", None),
    )
    out_specs = (
        P("dp", "context", None),
        P("dp", "context", None),
        P("context", None),
        P("context", None),
    )
    return jax.shard_map(
        on_device, mesh=mesh, in_specs=in_specs, out_specs=out_specs, check_vma=False
    )
```

```python
import functools

import jax
import jax.numpy as jnp
from jax import lax
from jax.experimental import pallas as pl
from jax.experimental.pallas import tpu as pltpu
from jax.sharding import PartitionSpec as P

CHUNKS = 8
LANES = 128
GROUP = 256
LOAD_PIECES = 1
VMEM_LIMIT = 24 * 1024 * 1024
STREAMS = ((5, "xyz", "yzx"), (8, "aybX", "yabX"))

TWO_OVER_PI = 0.6366197723675814
PIO2_HIGH = 1.5703125
PIO2_MID = 0.0004837512969970703
PIO2_LOW = 7.549789948768648e-08


def sin_cos(angle):
    quadrant_real = jnp.floor(angle * TWO_OVER_PI + 0.5)
    rest = angle - quadrant_real * PIO2_HIGH
    rest = rest - quadrant_real * PIO2_MID
    rest = rest - quadrant_real * PIO2_LOW
    square = rest * rest
    sine = rest + rest * square * (
        -1.6666654611e-1 + square * (8.3321608736e-3 + square * -1.9515295891e-4)
    )
    cosine = (
        1.0
        - 0.5 * square
        + square
        * square
        * (4.166664568298827e-2 + square * (-1.388731625493765e-3 + square * 2.443315711809948e-5))
    )
    quadrant = quadrant_real.astype(jnp.int32)
    swapped = (quadrant & 1) == 1
    sin_base = jnp.where(swapped, cosine, sine)
    cos_base = jnp.where(swapped, sine, cosine)
    sin_value = jnp.where((quadrant & 2) == 2, -sin_base, sin_base)
    cos_value = jnp.where(((quadrant + 1) & 2) == 2, -cos_base, cos_base)
    return sin_value, cos_value


def gain_of(decay):
    twice = 2.0 * decay
    series = 1.0 / 3628800.0
    for factorial in (362880.0, 40320.0, 5040.0, 720.0, 120.0, 24.0, 6.0, 2.0, 1.0):
        series = 1.0 / factorial - twice * series
    return jnp.sqrt(jnp.where(twice < 0.5, twice * series, 1.0 - jnp.exp(-twice)))


def places():
    return lax.axis_index("context"), lax.axis_index("dp")


def shuffle(back=False):
    length = GROUP // CHUNKS
    scan = lax.broadcasted_iota(jnp.int32, (GROUP, GROUP), 1 if back else 0)
    time = lax.broadcasted_iota(jnp.int32, (GROUP, GROUP), 0 if back else 1)
    return jnp.where(time == (scan % CHUNKS) * length + scan // CHUNKS, 1.0, 0.0).astype(
        jnp.bfloat16
    )


def local_scan_kernel(
    step_hbm,
    decay_hbm,
    frequency_hbm,
    in_hbm,
    cot_hbm,
    in_proj_hbm,
    out_proj_hbm,
    lam_re,
    lam_im,
    drive,
    adjoint,
    chunk_ref,
    summary_ref,
    outside_ref,
    in_vmem,
    cot_vmem,
    in_proj_vmem,
    out_proj_vmem,
    decay_ref,
    step_ref,
    frequency_ref,
    in_time,
    cot_time,
    sems,
):
    rows = in_vmem.shape[0]
    groups = rows // GROUP
    length = GROUP // CHUNKS
    states = decay_ref.shape[1]
    small = [
        pltpu.make_async_copy(source, target, sems.at[slot])
        for slot, (source, target) in enumerate(
            ((step_hbm, step_ref), (decay_hbm, decay_ref), (frequency_hbm, frequency_ref))
        )
    ]
    loads = []
    for array, (source, target) in enumerate(
        (
            (in_hbm, in_time),
            (in_proj_hbm, in_proj_vmem),
            (cot_hbm, cot_time),
            (out_proj_hbm, out_proj_vmem),
        )
    ):
        count = source.shape[0] // LOAD_PIECES
        loads.append(
            [
                pltpu.make_async_copy(
                    source.at[pl.ds(piece * count, count)],
                    target.at[pl.ds(piece * count, count)],
                    sems.at[3 + array * LOAD_PIECES + piece],
                )
                for piece in range(LOAD_PIECES)
            ]
        )
    for copy in small + [copy for load in loads[:2] for copy in load]:
        copy.start()
    for copy in small:
        copy.wait()
    decay = decay_ref[...]
    frequency = frequency_ref[...]
    gain = gain_of(decay)
    steps = [
        jnp.concatenate(
            [
                step_ref[:, first : first + length]
                for first in range(group * GROUP, (group + 1) * GROUP, length)
            ],
            axis=0,
        )
        for group in range(groups)
    ]
    for place in range(length):
        for group in range(groups):
            here = jnp.broadcast_to(steps[group][:, place : place + 1], (CHUNKS, states))
            damping = jnp.exp(-here * decay)
            sine, cosine = sin_cos(here * frequency)
            tile = pl.ds(group * GROUP + place * CHUNKS, CHUNKS)
            lam_re[tile, :] = damping * cosine
            lam_im[tile, :] = damping * sine
    for copy in [copy for load in loads[2:] for copy in load]:
        copy.start()
    to_scan = shuffle()
    pair_gain = jnp.concatenate([gain, gain], axis=1)
    for load, time_ref, scan_ref, proj_ref, target in (
        (loads[:2], in_time, in_vmem, in_proj_vmem, drive),
        (loads[2:], cot_time, cot_vmem, out_proj_vmem, adjoint),
    ):
        for copy in load[0]:
            copy.wait()
        for group in range(groups):
            part = pl.ds(group * GROUP, GROUP)
            scan_ref[part, :] = jnp.dot(
                to_scan, time_ref[part, :], preferred_element_type=jnp.float32
            ).astype(jnp.bfloat16)
        for copy in load[1]:
            copy.wait()
        driven = jnp.dot(scan_ref[...], proj_ref[...], preferred_element_type=jnp.float32)
        target[...] = driven * pair_gain if target is drive else driven
    re_cols, im_cols = pl.ds(0, states), pl.ds(states, states)

    def body(place, carry):
        results = []
        for group in range(groups):
            a_re, a_im, f_re, f_im, b_re, b_im = carry[6 * group : 6 * group + 6]
            first = group * GROUP + place * CHUNKS
            tile = pl.ds(pl.multiple_of(first, CHUNKS), CHUNKS)
            lam = lam_re[tile, :], lam_im[tile, :]
            a_re, a_im = times(lam, (a_re, a_im))
            f_re, f_im = plus(times(lam, (f_re, f_im)), (drive[tile, re_cols], drive[tile, im_cols]))
            added = times_conj((a_re, a_im), (adjoint[tile, re_cols], adjoint[tile, im_cols]))
            results += [a_re, a_im, f_re, f_im, b_re + added[0], b_im + added[1]]
        return tuple(results)

    zero = jnp.zeros((CHUNKS, states), jnp.float32)
    one = jnp.ones((CHUNKS, states), jnp.float32)
    totals = lax.fori_loop(0, length, body, (one, zero, zero, zero, zero, zero) * groups, unroll=4)
    parts = [totals[6 * group : 6 * group + 6] for group in range(groups)]
    for group in range(groups):
        for slot, part in enumerate(parts[group]):
            chunk_ref[slot, pl.ds(group * CHUNKS, CHUNKS), :] = part
    rows_of = [
        [part[chunk : chunk + 1, :] for part in parts[group]]
        for group in range(groups)
        for chunk in range(CHUNKS)
    ]
    t_are, t_aim, t_re, t_im = rows_of[0][:4]
    for l_re, l_im, d_re, d_im, _, _ in rows_of[1:]:
        t_are, t_aim = l_re * t_are - l_im * t_aim, l_re * t_aim + l_im * t_are
        t_re, t_im = l_re * t_re - l_im * t_im + d_re, l_re * t_im + l_im * t_re + d_im
    u_re, u_im = rows_of[-1][4:]
    for l_re, l_im, _, _, d_re, d_im in rows_of[-2::-1]:
        u_re, u_im = l_re * u_re + l_im * u_im + d_re, l_re * u_im - l_im * u_re + d_im
    summary_ref[...] = jnp.concatenate(
        [t_are, t_aim, t_re, t_im, u_re, u_im, t_are, t_aim], axis=0
    )
    one, zero = jnp.ones_like(t_are), jnp.zeros_like(t_are)
    outside_ref[...] = jnp.concatenate([one, zero, zero, zero] * 2, axis=0)


def held(shape, dtype=jnp.float32):
    return pltpu.VMEM(shape, dtype)


def call(kernel, name, out_shape, *args, inputs=None, outputs=None, scratch=(), flops=0):
    vmem = pl.BlockSpec(memory_space=pltpu.VMEM)
    return pl.pallas_call(
        kernel,
        out_shape=out_shape,
        in_specs=inputs or [vmem] * len(args),
        out_specs=outputs or jax.tree.map(lambda _: vmem, out_shape),
        scratch_shapes=scratch,
        compiler_params=pltpu.CompilerParams(vmem_limit_bytes=VMEM_LIMIT),
        cost_estimate=pl.CostEstimate(
            flops=flops, bytes_accessed=max(flops // 1000, 1024), transcendentals=0
        ),
        name=name,
    )(*args)


def local_scan(step_row, decay, frequency, flat_in, flat_cot, input_proj, output_proj):
    rows = flat_in.shape[0]
    states = decay.shape[1]
    args = [
        pltpu.with_memory_space_constraint(array, pltpu.HBM)
        for array in (step_row, decay, frequency, flat_in, flat_cot, input_proj, output_proj)
    ]
    return call(
        local_scan_kernel,
        "local_scan",
        [held((rows, states))] * 2
        + [held((rows, 2 * states))] * 2
        + [held((6, rows // GROUP * CHUNKS, states)), held((8, states)), held((8, states))]
        + [held(array.shape, array.dtype) for array in args[3:]]
        + [held(decay.shape)],
        *args,
        inputs=[pl.BlockSpec(memory_space=pltpu.HBM)] * 7,
        scratch=[
            pltpu.VMEM(step_row.shape, jnp.float32),
            pltpu.VMEM(frequency.shape, jnp.float32),
            pltpu.VMEM(flat_in.shape, flat_in.dtype),
            pltpu.VMEM(flat_cot.shape, flat_cot.dtype),
            pltpu.SemaphoreType.DMA((3 + 4 * LOAD_PIECES,)),
        ],
        flops=4 * rows * flat_in.shape[1] * 2 * states,
    )


def planes_kernel(skipped, lam_re, lam_im, drive, adjoint, *rest):
    fwd_re, fwd_im, fwd_are, fwd_aim, back_re, back_im, back_are, back_aim = rest[skipped:]
    rows, states = lam_re.shape
    groups, length = rows // GROUP, GROUP // CHUNKS
    re_cols, im_cols = pl.ds(0, states), pl.ds(states, states)

    def body(place, carry):
        results = []
        for group in range(groups):
            f_are, f_aim, f_re, f_im, b_are, b_aim, b_re, b_im = carry[8 * group : 8 * group + 8]
            first = group * GROUP + place * CHUNKS
            tile = pl.ds(pl.multiple_of(first, CHUNKS), CHUNKS)
            l_re, l_im = lam_re[tile, :], lam_im[tile, :]
            new_are = l_re * f_are - l_im * f_aim
            new_aim = l_re * f_aim + l_im * f_are
            new_re = l_re * f_re - l_im * f_im + drive[tile, re_cols]
            new_im = l_re * f_im + l_im * f_re + drive[tile, im_cols]
            fwd_are[tile, :] = new_are
            fwd_aim[tile, :] = new_aim
            fwd_re[tile, :] = new_re
            fwd_im[tile, :] = new_im
            first = group * GROUP + (length - 1 - place) * CHUNKS
            tile = pl.ds(pl.multiple_of(first, CHUNKS), CHUNKS)
            l_re, l_im = lam_re[tile, :], lam_im[tile, :]
            a_re = b_re + adjoint[tile, re_cols]
            a_im = b_im + adjoint[tile, im_cols]
            back_are[tile, :] = b_are
            back_aim[tile, :] = b_aim
            back_re[tile, :] = a_re
            back_im[tile, :] = a_im
            results += [
                new_are,
                new_aim,
                new_re,
                new_im,
                l_re * b_are + l_im * b_aim,
                l_re * b_aim - l_im * b_are,
                l_re * a_re + l_im * a_im,
                l_re * a_im - l_im * a_re,
            ]
        return tuple(results)

    zero = jnp.zeros((CHUNKS, states), jnp.float32)
    one = jnp.ones((CHUNKS, states), jnp.float32)
    lax.fori_loop(
        0, length, body, (one, zero, zero, zero, one, zero, zero, zero) * groups, unroll=4
    )


def planes_of(lam_re, lam_im, drive, adjoint, *after):
    vmem = pl.BlockSpec(memory_space=pltpu.VMEM)
    return call(
        functools.partial(planes_kernel, len(after)),
        "planes",
        [held(lam_re.shape)] * 8,
        lam_re,
        lam_im,
        drive,
        adjoint,
        *after,
        inputs=[vmem] * 4 + [pl.BlockSpec(memory_space=pl.ANY)] * len(after),
    )


def times(a, b):
    return a[0] * b[0] - a[1] * b[1], a[0] * b[1] + a[1] * b[0]


def times_conj(a, b):
    return a[0] * b[0] + a[1] * b[1], a[0] * b[1] - a[1] * b[0]


def plus(a, b):
    return a[0] + b[0], a[1] + b[1]


def pick(upper, a, b):
    return tuple(jnp.where(upper, x, y) for x, y in zip(a, b))


def pairs_of(array):
    return [(array[row : row + 1], array[row + 1 : row + 2]) for row in range(0, 8, 2)]


def widen(bit, outside, other):
    upper = ((lax.axis_index("context") >> bit) & 1) == 1
    below, below_sum, above, above_sum = outside
    product, forward, backward, _ = other
    return (
        pick(upper, times(below, product), below),
        pick(upper, plus(times(below, forward), below_sum), below_sum),
        pick(upper, above, times(above, product)),
        pick(upper, above_sum, plus(times_conj(above, backward), above_sum)),
    )


def combine_kernel(bit, total_ref, outside_ref, other_ref, total_out, outside_out):
    other = pairs_of(other_ref[...])
    mine = pairs_of(total_ref[...])
    outside = widen(bit, pairs_of(outside_ref[...]), other)
    outside_out[...] = jnp.concatenate([part for pair in outside for part in pair], axis=0)
    upper = ((lax.axis_index("context") >> bit) & 1) == 1
    low = [pick(upper, theirs, ours) for theirs, ours in zip(other, mine)]
    high = [pick(upper, ours, theirs) for theirs, ours in zip(other, mine)]
    product = times(low[0], high[0])
    forward = plus(times(high[0], low[1]), high[1])
    backward = plus(times_conj(low[0], high[2]), low[2])
    total_out[...] = jnp.concatenate([*product, *forward, *backward, *product], axis=0)


def pairs_into(forward, chunk_ref, outside, gain, re_ref, im_ref, are_ref, aim_ref, pairs_ref):
    rows, states = re_ref.shape
    groups = rows // GROUP
    c_re, c_im = outside[1] if forward else outside[3]
    starts = {}
    chunks = range(groups * CHUNKS)
    for chunk in chunks if forward else reversed(chunks):
        starts[chunk] = (c_re, c_im)
        part = lambda slot: chunk_ref[slot, chunk : chunk + 1, :]
        factor, added = (part(0), part(1)), (part(2), part(3)) if forward else (part(4), part(5))
        c_re, c_im = plus((times if forward else times_conj)(factor, (c_re, c_im)), added)
    for group in range(groups):
        mine = [starts[group * CHUNKS + chunk] for chunk in range(CHUNKS)]
        c_re = jnp.concatenate([start[0] for start in mine] * 2, axis=0)
        c_im = jnp.concatenate([start[1] for start in mine] * 2, axis=0)
        for first in range(group * GROUP, (group + 1) * GROUP, 2 * CHUNKS):
            part = pl.ds(first, 2 * CHUNKS)
            a_re, a_im = are_ref[part, :], aim_ref[part, :]
            s_re = re_ref[part, :] + a_re * c_re - a_im * c_im
            s_im = im_ref[part, :] + a_re * c_im + a_im * c_re
            if not forward:
                s_re, s_im = s_re * gain, s_im * gain
            pairs_ref[part, pl.ds(0, states)] = s_re.astype(jnp.bfloat16)
            pairs_ref[part, pl.ds(states, states)] = s_im.astype(jnp.bfloat16)


def side_kernel(own, bit, parts, skipped, *refs):
    decay_ref, chunk_ref, *planes_refs = refs[:10]
    outside_ref, other_ref, in_ref, cot_ref = refs[10:14]
    pairs_ref, *outs, grad_ref = refs[14 + skipped :]
    core = places()[1] & 1
    of_input = core == (0 if own else 1)
    outside = widen(bit, pairs_of(outside_ref[...]), pairs_of(other_ref[...]))
    over_rows = (((0,), (0,)), ((), ()))
    for forward, rows_ref, planes in (
        (True, cot_ref, planes_refs[:4]),
        (False, in_ref, planes_refs[4:]),
    ):

        @pl.when(of_input != forward)
        def _():
            gain = gain_of(decay_ref[...])
            pairs_into(forward, chunk_ref, outside, gain, *planes, pairs_ref)
            grad_ref[...] = lax.dot_general(
                rows_ref[...], pairs_ref[...], over_rows, preferred_element_type=jnp.float32
            ).reshape(grad_ref.shape)

    for (layout, steps, far, first, past), out in zip(parts, outs):
        for block, both in enumerate(
            zip(*(block_indices(layout, [], step, far) for step in steps[::-1]))
        ):
            out[block] = grad_ref[jnp.where(core == 0, *both), first:past, :]


def side(own, bit, parts, piece, decay, chunk_totals, planes, outside, other, flat_in, flat_cot, after):
    rows, width = flat_in.shape
    states = decay.shape[1]
    args = [decay, chunk_totals, *planes, outside, other, flat_in, flat_cot, *after]
    blocks = (width // piece, piece, 2 * states)
    vmem = pl.BlockSpec(memory_space=pltpu.VMEM)
    shapes = [held((rows, 2 * states), jnp.bfloat16)]
    if own:
        shapes.append(held(blocks))
    for _, steps, _, first, past in parts:
        count = blocks[0] if steps[0] is None else blocks[0] // 2
        shapes.append(held((count, past - first, 2 * states)))
    return call(
        functools.partial(side_kernel, own, bit, parts, len(after)),
        "kept" if own else "lent",
        shapes,
        *args,
        inputs=[vmem] * (len(args) - len(after)) + [pl.BlockSpec(memory_space=pl.ANY)] * len(after),
        scratch=() if own else (pltpu.VMEM(blocks, jnp.float32),),
        flops=2 * rows * width * 2 * states,
    )


def products_kernel(
    in_ref,
    cot_ref,
    lent_ref,
    kept_ref,
    in_proj_ref,
    out_proj_ref,
    skip_ref,
    after_ref,
    out_hbm,
    back_hbm,
    token_ref,
    out_ref,
    back_ref,
    sems,
):
    token_ref[...] = jnp.zeros_like(token_ref)
    over_states = (((1,), (1,)), ((), ()))
    skip = skip_ref[...]
    to_time = shuffle(back=True)
    core = places()[1] & 1
    stores = [
        pltpu.make_async_copy(out_ref, out_hbm, sems.at[0]),
        pltpu.make_async_copy(back_ref, back_hbm, sems.at[1]),
    ]
    for slot, (proj, skipped, target) in enumerate(
        ((out_proj_ref, in_ref, out_ref), (in_proj_ref, cot_ref, back_ref))
    ):
        for which, pairs in enumerate((lent_ref, kept_ref)):

            @pl.when((core == slot) == (which == 0))
            def _():
                mixed = lax.dot_general(
                    pairs[...], proj[...], over_states, preferred_element_type=jnp.float32
                )
                mixed = (mixed + skip * skipped[...].astype(jnp.float32)).astype(jnp.bfloat16)
                for first in range(0, mixed.shape[0], GROUP):
                    target[pl.ds(first, GROUP), :] = jnp.dot(
                        to_time, mixed[first : first + GROUP], preferred_element_type=jnp.float32
                    ).astype(jnp.bfloat16)

        stores[slot].start()
    for store in stores:
        store.wait()


def products(
    flat_in, flat_cot, lent_pairs, kept_pairs, input_proj, output_proj, skip_gain, after
):
    rows, width = flat_in.shape
    vmem = pl.BlockSpec(memory_space=pltpu.VMEM)
    hbm = pl.BlockSpec(memory_space=pltpu.HBM)
    return call(
        products_kernel,
        "products",
        [
            jax.ShapeDtypeStruct(flat_in.shape, jnp.bfloat16),
            jax.ShapeDtypeStruct(flat_in.shape, jnp.bfloat16),
            held((8, LANES)),
        ],
        flat_in,
        flat_cot,
        lent_pairs,
        kept_pairs,
        input_proj,
        output_proj,
        skip_gain,
        after,
        inputs=[vmem] * 7 + [pl.BlockSpec(memory_space=pl.ANY)],
        outputs=[hbm, hbm, vmem],
        scratch=[
            pltpu.VMEM(flat_in.shape, jnp.bfloat16),
            pltpu.VMEM(flat_in.shape, jnp.bfloat16),
            pltpu.SemaphoreType.DMA((2,)),
        ],
        flops=4 * rows * width * lent_pairs.shape[1],
    )


def own_bit(step):
    axis, bit = step
    return (lax.axis_index(axis) >> bit) & 1


def block_indices(layout, settled, sent, far, sources=None):
    values = {step: own_bit(step) for step in settled}
    if sent is not None:
        values[sent] = 1 - own_bit(sent) if far else own_bit(sent)
    free = [step for step in layout if step not in values]
    found = []
    for block in range(2 ** len(free)):
        for place, step in enumerate(free):
            values[step] = (block >> (len(free) - 1 - place)) & 1
        indices = []
        for source in sources or [layout]:
            index = 0
            for step in source:
                index = index * 2 + values[step]
            indices.append(index)
        found.append(indices if sources else indices[0])
    return found


def add_kernel(layout, layouts, rows, settled, sent, scale, count, *refs):
    sources, out = refs[:count], refs[-1]
    is_zero = (lax.axis_index("dp") & 1) == 0
    indices = [
        block_indices(layout, settled[core], sent[core], True, layouts[core]) for core in range(2)
    ]
    for block, both in enumerate(zip(*indices)):
        total = None
        for source, zero, one in zip(sources, *both):
            index = jnp.where(is_zero, zero, one)
            whole = source.shape[1] == rows[1] - rows[0]
            part = source[index] if whole else source[index, rows[0] : rows[1], :]
            total = part if total is None else total + part
        out[block] = total if scale is None else total * scale


def gather_kernel(items, *refs):
    in_ref, out_ref = refs[-2:]
    dp_place = places()[1]
    for (rows, offset), share in zip(items, refs[:-2]):
        place = dp_place ^ offset
        for core, target in enumerate((in_ref, out_ref)):

            @pl.when(place & 1 == core)
            def _():
                if share.shape[0] == target.shape[0]:
                    target[:, rows[0] : rows[1], :] = share[...]
                else:
                    target[place >> 1, rows[0] : rows[1], :] = share[0]


def on_device(
    inputs, step_size, decay_rate, frequency, input_proj, output_proj, skip_gain, cotangent
):
    batch_count, row_count, model_width = inputs.shape
    state_count = decay_rate.shape[0]
    dp_count, context_count = lax.axis_size("dp"), lax.axis_size("context")
    dp_bits, context_bits = dp_count.bit_length() - 1, context_count.bit_length() - 1

    def swap(array, *steps):
        pairs = []
        for dp in range(dp_count):
            axis, bit = steps[dp & (len(steps) - 1)]
            for context in range(context_count):
                if axis == "dp":
                    partner = (dp ^ (1 << bit)) * context_count + context
                else:
                    partner = dp * context_count + (context ^ (1 << bit))
                pairs.append((dp * context_count + context, partner))
        return lax.ppermute(array, ("dp", "context"), pairs)

    *driven, chunk_totals, total, outside, flat_in, flat_cot, in_proj, out_proj, decay = local_scan(
        step_size,
        decay_rate.reshape(1, state_count),
        frequency.reshape(1, state_count),
        inputs.reshape(row_count, model_width),
        cotangent.reshape(row_count, model_width),
        input_proj,
        output_proj,
    )
    for bit in range(context_bits - 1):
        other = swap(total, ("context", bit))
        total, outside = call(
            functools.partial(combine_kernel, bit),
            "combine",
            [held(total.shape), held(outside.shape)],
            total,
            outside,
            other,
        )
    planes = planes_of(*driven, outside)
    last = context_bits - 1
    other = swap(total, ("context", last))

    extra_bits = [("dp", bit) for bit in range(1, dp_bits)]
    z_bits = [("context", bit) for bit in range(1, context_bits)]
    by_name = {
        "x": extra_bits,
        "y": [("context", 0)],
        "z": z_bits,
        "a": z_bits[:1],
        "b": z_bits[1:],
    }
    layout = [("context", bit) for bit in reversed(range(context_bits))] + extra_bits[::-1]
    piece = model_width // 2 ** len(layout)
    grad_scale = float(batch_count * row_count * dp_count * context_count) ** (-0.5)
    less = lambda taken: [step for step in layout if step not in taken]
    streams, first, parts = [], 0, []
    for eighths, *names in STREAMS:
        past = max(8, piece * eighths // 64 * 8)
        if past > first:
            orders = [[step for name in order for step in by_name[name.lower()]] for order in names]
            halvings = len(layout) - (len(extra_bits) if "X" in names[0] else 0)
            streams.append(
                {"rows": (first, past), "orders": orders, "settled": ([], []), "halvings": halvings}
            )
            steps = [order[0] for order in orders]
            pieces = [(steps, True), (steps, False)] if first == 0 else [((None, None), False)]
            parts += [(layout, which, far, first, past) for which, far in pieces]
            first = past

    common = (decay, chunk_totals, planes, outside, other, flat_in, flat_cot)
    lent_pairs, *lent = side(False, last, parts, piece, *common, ())
    borrowed = [swap(part, ("dp", 0)) for part in lent]
    kept_pairs, kept = side(True, last, [], piece, *common, lent[:1])

    vmem, anywhere = pl.BlockSpec(memory_space=pltpu.VMEM), pl.BlockSpec(memory_space=pl.ANY)

    def add(stream, sources, sent=(None, None), scale=None, later=()):
        layouts = [[left[core] for _, left in sources] for core in range(2)]
        free = len(layout) - len(stream["settled"][0]) - (sent[0] is not None)
        first, past = stream["rows"]
        return call(
            functools.partial(
                add_kernel,
                layout,
                layouts,
                stream["rows"],
                stream["settled"],
                sent,
                scale,
                len(sources),
            ),
            "halve" if scale is None else "share",
            held((2**free, past - first, 2 * state_count)),
            *(source for source, _ in sources),
            *later,
            inputs=[vmem] * len(sources) + [anywhere] * len(later),
        )

    before = []
    for place in range(len(layout)):
        for number, stream in enumerate(streams):
            steps = [order[place] for order in stream["orders"]]
            if place >= stream["halvings"]:
                left = tuple(less(settled) for settled in stream["settled"])
                away = add(stream, stream["sources"], later=before)
                stream["sources"] = [(away, left), (swap(away, *steps), left)]
                continue
            if place == 0:
                left = tuple(less([step]) for step in steps)
                if number == 0:
                    far, near = borrowed[:2]
                else:
                    far, near, left = borrowed[number + 1], borrowed[number + 1], (layout, layout)
                stream["sources"] = [(kept, (layout, layout)), (near, left)]
                away = add(stream, [stream["sources"][0], (far, left)], steps, later=before)
            else:
                away = add(stream, stream["sources"], steps, later=before)
            stream["settled"] = tuple(
                settled + [step] for settled, step in zip(stream["settled"], steps)
            )
            left = tuple(less(settled) for settled in stream["settled"])
            stream["sources"] = stream["sources"] + [(swap(away, *steps), left)]
        if place == 0:
            outputs, input_grad, token = products(
                flat_in,
                flat_cot,
                lent_pairs,
                kept_pairs,
                in_proj,
                out_proj,
                skip_gain.reshape(1, model_width),
                away,
            )
            before = [token]
    items, shares = [], []
    for stream in streams:
        mine = [(0, add(stream, stream["sources"], scale=grad_scale, later=before))]
        before = ()
        for bit in [bit for _, bit in extra_bits if stream["halvings"] == len(layout)] + [0]:
            mine = mine + [
                (offset ^ (1 << bit), swap(share, ("dp", bit))) for offset, share in mine
            ]
        for offset, share in mine:
            items.append((stream["rows"], offset))
            shares.append(share)
    whole = jax.ShapeDtypeStruct((dp_count // 2, piece, 2 * state_count), jnp.float32)
    sums = call(functools.partial(gather_kernel, items), "gather", [whole, whole], *shares)
    sums = [part.reshape(model_width // context_count, 2 * state_count) for part in sums]
    return (outputs.reshape(inputs.shape), input_grad.reshape(inputs.shape), *sums)


def solution(mesh):
    in_specs = (
        P("dp", "context", None),
        P("dp", "context"),
        P(),
        P(),
        P(),
        P(),
        P(),
        P("dp", "context", None),
    )
    out_specs = (
        P("dp", "context", None),
        P("dp", "context", None),
        P("context", None),
        P("context", None),
    )
    return jax.shard_map(
        on_device, mesh=mesh, in_specs=in_specs, out_specs=out_specs, check_vma=False
    )
```
